256 devices in a mesh: grp: 8 (over y, z_lo), own: 32 (over z_hi, x, core).
Axes of the slice: x: 4, y: 4, z: 8 (z_hi: 4, z_lo: 2; z = z_hi * 2 + z_lo), core: 2. Of those that a mesh axis runs over, the one named last changes fastest.
Arguments:
- particles: bfloat16 [512, 256, 256], P(('grp', 'own')), may hold values from -8 to 8
- inv_noise: float32 [512], P(('grp', 'own')), may hold values from 0.02 to 0.06
- class_images: bfloat16 [128, 256, 256], P('own'), may hold values from -8 to 8
- col_factor: bfloat16 [256, 4096], replicated, may hold values from -0.375 to 0.375
- row_factor: bfloat16 [256, 4096], replicated, may hold values from -0.375 to 0.375
- row_shifts: int32 [3], replicated, may hold values from -6 to 6, as said below
- col_shifts: int32 [3], replicated, may hold values from -6 to 6, as said below
Outputs:
- new_averages: float32 [128, 4096], P('own')
- occupancy: float32 [128], P('own')
The draws below stay inside these ranges and needn't reach their ends.
Inputs may be any that keep to these rules, and one draw needn't show every extreme that they name: `row_shifts`: the row offsets include -6 and 6. `col_shifts`: the column offsets include -6 and 6.
All inputs are finite; a program needn't handle non-finite values.
Results may differ from the reference program's by a relative error of at most 0.0028.
Values may be sent and summed in bfloat16 or wider, within the bound.
A program may use at most 64 MiB of HBM per device.

```python
import math
import jax
import jax.numpy as jnp
from jax import lax

IMAGE_SIDE = 256
POLAR_CYCLES = 32
POLAR_ANGLES = 128
POLAR_SIZE = 4096
SHIFT_SIDE = 3
CLASSES = 128
PART_DEV = 2
PARTICLES = 512


def offset_list(key):
    middle = jax.random.randint(jax.random.fold_in(key, 5), (SHIFT_SIDE - 2,), -5, 6, dtype=jnp.int32)
    values = jnp.concatenate([jnp.array([-6, 6], jnp.int32), middle])
    return jax.random.permutation(jax.random.fold_in(key, 9), values)


def shared_offsets(key):
    base_key = jax.random.fold_in(key, 171)
    rows = offset_list(jax.random.fold_in(base_key, 11))
    cols = offset_list(jax.random.fold_in(base_key, 12))
    return jnp.stack([rows, cols])


def shared_classes(key):
    inner_key = jax.random.fold_in(key, 72)
    return jax.random.normal(inner_key, (CLASSES, IMAGE_SIDE, IMAGE_SIDE), jnp.float32)


def draw_row_shifts(key, part):
    return shared_offsets(key)[0]


def draw_col_shifts(key, part):
    return shared_offsets(key)[1]


def draw_class_images(key, part):
    return shared_classes(key).astype(jnp.bfloat16)


def draw_particles(key, part):
    inner_key = jax.random.fold_in(key, 73)
    noise_field = jax.random.normal(inner_key, (PARTICLES, IMAGE_SIDE, IMAGE_SIDE), jnp.float32)
    return noise_field.astype(jnp.bfloat16)


def level_of(key, extent, cuts, low, high):
    loudness = 1.0
    for position, parts in cuts:
        draws = jax.random.uniform(jax.random.fold_in(jax.random.fold_in(key, 6), position), (parts,), jnp.float32, low / len(cuts), high / len(cuts))
        loudness = loudness * jnp.repeat(jnp.exp(draws), extent[position] // parts).reshape((-1,) + (1,) * (len(extent) - 1 - position))
    return loudness


def noise(stream_key, extent, width, reach, kind=jnp.bfloat16):
    return jnp.clip(width * jax.random.normal(stream_key, extent, jnp.float32), -reach, reach).astype(kind)


def setup_inputs(seed: int = 0) -> dict:
    keys = jax.random.split(jax.random.key(seed), 8)
    return {
        "particles": draw_particles(jax.random.fold_in(keys[7], 71), 0),
        "inv_noise": jnp.clip(jnp.exp(math.log(0.06) - 1.0986123 * jax.random.uniform(keys[1], (PARTICLES,), jnp.float32) ** level_of(keys[1], (PARTICLES,), ((0, 256),), -0.2, 0.2)), 0.02, 0.06),
        "class_images": draw_class_images(jax.random.fold_in(keys[7], 71), 0),
        "col_factor": noise(keys[3], (IMAGE_SIDE, POLAR_SIZE), IMAGE_SIDE ** -0.5, 0.375),
        "row_factor": noise(keys[4], (IMAGE_SIDE, POLAR_SIZE), IMAGE_SIDE ** -0.5, 0.375),
        "row_shifts": draw_row_shifts(jax.random.fold_in(keys[7], 71), 0),
        "col_shifts": draw_col_shifts(jax.random.fold_in(keys[7], 71), 0),
    }


def spread_rows(images, col_factor):
    flat = images.reshape(-1, images.shape[-1])
    product = jnp.dot(flat, col_factor, preferred_element_type=jnp.float32)
    return product.reshape(images.shape[0], images.shape[1], col_factor.shape[1])


def reference(particles, inv_noise, class_images, col_factor, row_factor, row_shifts, col_shifts):
    row_plain = row_factor.astype(jnp.float32)

    def class_polar(picture):
        spread = jnp.dot(picture, col_factor, preferred_element_type=jnp.float32)
        return jnp.sum(spread * row_plain, axis=0)

    own_polar = lax.map(class_polar, class_images).astype(jnp.bfloat16)
    classes = own_polar.astype(jnp.float32).reshape(CLASSES, POLAR_CYCLES, POLAR_ANGLES)
    class_norms = jnp.sum(classes * classes, axis=(1, 2))
    class_hat = jnp.fft.fft(classes, axis=2)
    row_moved = [jnp.roll(row_factor, -row_shifts[row_index], axis=0).astype(jnp.float32) for row_index in range(SHIFT_SIDE)]

    def particle_polar(picture):
        shifted = jnp.stack([jnp.roll(picture, col_shifts[col_index], axis=1) for col_index in range(SHIFT_SIDE)])
        spread = spread_rows(shifted, col_factor)
        stacked = jnp.stack([jnp.sum(spread * row_moved[row_index], axis=1) for row_index in range(SHIFT_SIDE)])
        return stacked.reshape(SHIFT_SIDE * SHIFT_SIDE, POLAR_SIZE)

    def one_block(carry, inputs):
        pictures, betas = inputs
        polar = lax.map(particle_polar, pictures).reshape(-1, POLAR_CYCLES, POLAR_ANGLES)
        polar_hat = jnp.fft.fft(polar, axis=2)
        cross_terms = jnp.einsum('srm,krm->skm', jnp.conj(polar_hat), class_hat)
        correlation = jnp.real(jnp.fft.ifft(cross_terms, axis=2))
        beta_rows = jnp.repeat(betas, SHIFT_SIDE * SHIFT_SIDE)
        scores = beta_rows[:, None, None] * (correlation - 0.5 * class_norms[None, :, None])
        grouped = scores.reshape(pictures.shape[0], -1)
        row_top = jnp.max(grouped, axis=1, keepdims=True)
        raised = jnp.exp(grouped - row_top)
        weights = (raised / jnp.sum(raised, axis=1, keepdims=True)).reshape(scores.shape)
        weight_hat = jnp.fft.fft(weights, axis=2)
        sum_hat = jnp.einsum('srm,skm->krm', polar_hat, weight_hat)
        class_sums = jnp.real(jnp.fft.ifft(sum_hat, axis=2)).reshape(CLASSES, POLAR_SIZE)
        class_mass = jnp.sum(weights, axis=(0, 2))
        return (carry[0] + class_sums, carry[1] + class_mass), None

    block_count = PARTICLES // PART_DEV
    pictures_all = particles.reshape(block_count, PART_DEV, IMAGE_SIDE, IMAGE_SIDE)
    betas_all = inv_noise.reshape(block_count, PART_DEV)
    start_sums = jnp.zeros((CLASSES, POLAR_SIZE), jnp.float32)
    start_mass = jnp.zeros((CLASSES,), jnp.float32)
    (class_sums, class_mass), _ = lax.scan(one_block, (start_sums, start_mass), (pictures_all, betas_all))
    new_averages = class_sums / jnp.maximum(class_mass, 1.0)[:, None]
    return (new_averages, class_mass)
```

```python
import functools

import jax
import jax.numpy as jnp
from jax import lax
from jax.experimental import pallas as pl
from jax.experimental.pallas import tpu as pltpu
from jax.sharding import PartitionSpec as P

F32 = jnp.float32
BF16 = jnp.bfloat16
ANGLES = 128
SHIFTS = 3
FINE = 8
COARSE = ANGLES // FINE
OWNED = 4
SUBS = 4
QUARTERS = 4
POLAR_TILE = 256
SUM_TILE = 512
MESH = pl.DeviceIdType.MESH


def contract_last(left, right):
    return lax.dot_general(left, right, (((1,), (1,)), ((), ())), preferred_element_type=F32)


def matmul(left, right):
    return jnp.dot(left, right, preferred_element_type=F32)


def kernel(
    layout,
    part_ref,
    noise_ref,
    cls_ref,
    col_ref,
    row_ref,
    rs_ref,
    cs_ref,
    sums_ref,
    mass_ref,
    pics,
    spread_a,
    spread_b,
    rowp,
    cp_f32,
    cp_all,
    pp_all,
    beta_all,
    stats,
    part_hi,
    part_lo,
    part_ninth,
    cls_roll,
    norm_acc,
    score_a,
    score_b,
    weight_a,
    weight_b,
    grid_a,
    grid_b,
    own_sum,
    x_send,
    x_recv,
    xm_send,
    xm_recv,
    y_send,
    y_recv,
    z_send,
    z_recv,
    gathered,
    pair_send_sem,
    pair_recv_sem,
    cz_send_sem,
    cz_recv_sem,
    cx_send_sem,
    cx_recv_sem,
    x_send_sem,
    x_recv_sem,
    xm_send_sem,
    xm_recv_sem,
    y_send_sem,
    y_recv_sem,
    z_send_sem,
    z_recv_sem,
    g_send_sem,
    g_recv_sem,
):
    xs, ys, zhs, zls = layout
    side = part_ref.shape[1]
    polar = col_ref.shape[1]
    cycles = polar // ANGLES
    width = polar // QUARTERS
    quarter_cycles = cycles // QUARTERS
    owners = xs * zhs
    local = OWNED * owners
    block_rows = OWNED * zhs
    y_width = polar // ys
    z_width = y_width // zls

    grp = lax.axis_index("grp")
    own = lax.axis_index("own")
    zl = grp % zls
    y = grp // zls
    core = own % 2
    x = (own // 2) % xs
    zh = own // (2 * xs)

    def device(y_at, zl_at, zh_at, x_at, core_at):
        return {"grp": y_at * zls + zl_at, "own": (zh_at * xs + x_at) * 2 + core_at}

    partner = device(y, zl, zh, x, 1 - core)

    def x_peer(step):
        return device(y, zl, zh, (x + step) % xs, core)

    def y_peer(step):
        return device((y + step) % ys, zl, zh, x, core)

    def z_peer(high, low):
        return device(y, (zl + low) % zls, (zh + high) % zhs, x, core)

    def g_peer(step_y, step_l):
        return device((y + step_y) % ys, (zl + step_l) % zls, zh, x, core)

    peers = [partner]
    peers += [x_peer(step) for step in range(1, xs)]
    peers += [z_peer(high, low) for high in range(zhs) for low in range(zls) if high or low]
    peers += [
        g_peer(step_y, step_l) for step_y in range(1, ys) for step_l in range(zls)
    ]
    barrier = pltpu.get_barrier_semaphore()
    for peer in peers:
        pl.semaphore_signal(barrier, inc=1, device_id=peer, device_id_type=MESH)

    def remote(src, dst, send_sem, recv_sem, peer):
        return pltpu.make_async_remote_copy(
            src_ref=src,
            dst_ref=dst,
            send_sem=send_sem,
            recv_sem=recv_sem,
            device_id=peer,
            device_id_type=MESH,
        )

    def class_spread(tile, store):
        store[0 : OWNED * side, :] = matmul(
            cls_ref[...].reshape(OWNED * side, side),
            col_ref[:, pl.ds(pl.multiple_of(tile * POLAR_TILE, POLAR_TILE), POLAR_TILE)],
        )

    def class_reduce(tile, quarter, store):
        for half in range(POLAR_TILE // ANGLES):
            at = pl.multiple_of(tile * POLAR_TILE + half * ANGLES, ANGLES)
            place = pl.multiple_of(at - quarter * width, ANGLES)
            lanes = slice(half * ANGLES, (half + 1) * ANGLES)
            totals = [jnp.zeros((8, ANGLES), F32)] * OWNED
            for block in range(side // 16):
                rows = row_ref[block * 16 : block * 16 + 16, pl.ds(at, ANGLES)].astype(F32)
                for sub in range(2):
                    for k in range(OWNED):
                        start = k * side + block * 16 + sub * 8
                        totals[k] = totals[k] + store[start : start + 8, lanes] * rows[sub * 8 : sub * 8 + 8]
            for k in range(OWNED):
                cp_f32[quarter * OWNED + k : quarter * OWNED + k + 1, pl.ds(place, ANGLES)] = jnp.sum(
                    totals[k], axis=0, keepdims=True
                )

    tiles_per_quarter = width // POLAR_TILE
    last_tile = polar // POLAR_TILE - 1
    class_spread(0, spread_a)
    for quarter in range(QUARTERS):

        def class_pair(step, carry):
            tile = quarter * tiles_per_quarter + 2 * step
            class_spread(tile + 1, spread_b)
            class_reduce(tile, quarter, spread_a)
            class_spread(jnp.minimum(tile + 2, last_tile), spread_a)
            class_reduce(tile + 1, quarter, spread_b)
            return carry

        lax.fori_loop(0, tiles_per_quarter // 2, class_pair, 0)
    cp_all[0, 0] = cp_f32[...].astype(BF16)

    pl.semaphore_wait(barrier, len(peers))
    waits = []

    def start(copy):
        copy.start()
        waits.append(copy)
        return copy

    gather_z = [None] + [
        start(
            remote(
                cp_all.at[0, 0],
                cp_all.at[0, high],
                cz_send_sem.at[high],
                cz_recv_sem.at[high],
                z_peer(high, 0),
            )
        )
        for high in range(1, zhs)
    ]
    gather_x = {}

    def forward(high):
        if high:
            gather_z[high].wait_recv()
        for step in range(1, xs):
            gather_x[step, high] = start(
                remote(
                    cp_all.at[0, high],
                    cp_all.at[step, high],
                    cx_send_sem.at[step, high],
                    cx_recv_sem.at[step, high],
                    x_peer(step),
                )
            )

    forward(0)

    beta_rows = lax.broadcasted_iota(jnp.int32, (8, ANGLES), 0)
    beta_all[core] = jnp.where(beta_rows == 0, noise_ref[0], noise_ref[1])
    beta_copy = start(
        remote(
            beta_all.at[core], beta_all.at[core], pair_send_sem.at[0], pair_recv_sem.at[0], partner
        )
    )

    from_col = lax.broadcasted_iota(jnp.int32, (side, side), 0)
    to_col = lax.broadcasted_iota(jnp.int32, (side, side), 1)
    for j in range(SHIFTS):
        mover = jnp.where(((to_col - cs_ref[j]) & (side - 1)) == from_col, 1.0, 0.0).astype(BF16)
        for n in range(2):
            start_row = (n * SHIFTS + j) * side
            pics[start_row : start_row + side, :] = matmul(part_ref[n], mover).astype(BF16)

    def extend(cycle, carry):
        at = pl.multiple_of(cycle * ANGLES, ANGLES)
        values = row_ref[:, pl.ds(at, ANGLES)].astype(F32)
        rowp[cycle, 8 : side + 8, :] = values
        rowp[cycle, 0:8, :] = values[side - 8 : side]
        rowp[cycle, side + 8 : side + 16, :] = values[0:8]
        return carry

    lax.fori_loop(0, cycles, extend, 0)

    offsets = [rs_ref[i] for i in range(SHIFTS)]

    def part_spread(tile, store):
        store[...] = matmul(
            pics[...],
            col_ref[:, pl.ds(pl.multiple_of(tile * POLAR_TILE, POLAR_TILE), POLAR_TILE)],
        )

    def part_reduce(tile, quarter, store):
        for half in range(POLAR_TILE // ANGLES):
            cycle = tile * (POLAR_TILE // ANGLES) + half
            place = pl.multiple_of((cycle - quarter * quarter_cycles) * ANGLES, ANGLES)
            lanes = slice(half * ANGLES, (half + 1) * ANGLES)
            totals = [jnp.zeros((8, ANGLES), F32)] * (2 * SHIFTS * SHIFTS)
            for block in range(side // 8):
                rows = [
                    rowp[cycle, pl.ds(8 + block * 8 + offsets[i], 8), :] for i in range(SHIFTS)
                ]
                for n in range(2):
                    for j in range(SHIFTS):
                        begin = (n * SHIFTS + j) * side + block * 8
                        value = store[begin : begin + 8, lanes]
                        for i in range(SHIFTS):
                            index = n * 9 + i * SHIFTS + j
                            totals[index] = totals[index] + value * rows[i]
            for n in range(2):
                for s in range(8):
                    pp_all[core, quarter, 8 * n + s : 8 * n + s + 1, pl.ds(place, ANGLES)] = jnp.sum(
                        totals[n * 9 + s], axis=0, keepdims=True
                    )
                ninth = jnp.broadcast_to(
                    jnp.sum(totals[n * 9 + 8], axis=0, keepdims=True), (8, ANGLES)
                )
                for sub in range(SUBS):
                    row = 16 + 2 * sub + n
                    moved = ninth if sub == 0 else pltpu.roll(ninth, sub * FINE, 1)
                    pp_all[core, quarter, row : row + 1, pl.ds(place, ANGLES)] = moved[0:1]

    pair_copies = []
    part_spread(0, spread_a)
    for quarter in range(QUARTERS):

        def part_pair(step, carry):
            tile = quarter * tiles_per_quarter + 2 * step
            part_spread(tile + 1, spread_b)
            part_reduce(tile, quarter, spread_a)
            part_spread(jnp.minimum(tile + 2, last_tile), spread_a)
            part_reduce(tile + 1, quarter, spread_b)
            return carry

        lax.fori_loop(0, tiles_per_quarter // 2, part_pair, 0)
        pair_copies.append(
            start(
                remote(
                    pp_all.at[core, quarter],
                    pp_all.at[core, quarter],
                    pair_send_sem.at[1 + quarter],
                    pair_recv_sem.at[1 + quarter],
                    partner,
                )
            )
        )
        if quarter == 1:
            for high in range(1, zhs):
                forward(high)

    def split_store(value, rows, at, high_ref, low_ref, low_rows):
        high = value.astype(BF16)
        high_ref[rows, pl.ds(at, ANGLES)] = high
        low_ref[low_rows, pl.ds(at, ANGLES)] = (value - high.astype(F32)).astype(BF16)

    ninth_rows = 16 * (COARSE // SUBS)
    for quarter in range(QUARTERS):
        pair_copies[quarter].wait_recv()

        def roll_particles(step, carry):
            lanes = pl.ds(pl.multiple_of(step * ANGLES, ANGLES), ANGLES)
            at = pl.multiple_of(quarter * width + step * ANGLES, ANGLES)
            first = pp_all[0, quarter, :, lanes]
            second = pp_all[1, quarter, :, lanes]
            eight = jnp.concatenate([first[0:16], second[0:16]], axis=0)
            ninth = jnp.concatenate([first[16:24], second[16:24]], axis=0)
            for coarse in range(COARSE):
                moved = eight if coarse == 0 else pltpu.roll(eight, coarse * FINE, 1)
                rows = slice(32 * coarse, 32 * coarse + 32)
                split_store(moved, rows, at, part_hi, part_lo, rows)
            for coarse in range(COARSE // SUBS):
                moved = ninth if coarse == 0 else pltpu.roll(ninth, coarse * FINE * SUBS, 1)
                rows = slice(16 * coarse, 16 * coarse + 16)
                low_rows = slice(ninth_rows + 16 * coarse, ninth_rows + 16 * coarse + 16)
                split_store(moved, rows, at, part_ninth, part_ninth, low_rows)
            return carry

        lax.fori_loop(0, quarter_cycles, roll_particles, 0)

    for step in range(1, xs):
        for high in range(zhs):
            gather_x[step, high].wait_recv()
    norm_acc[...] = jnp.zeros_like(norm_acc)
    sub_index = lax.broadcasted_iota(jnp.int32, (owners // 2, 8, ANGLES), 1)
    for quarter in range(QUARTERS):

        def roll_classes(step, carry):
            lanes = pl.ds(pl.multiple_of(step * ANGLES, ANGLES), ANGLES)
            at = pl.multiple_of(quarter * width + step * ANGLES, ANGLES)
            raw = cp_all[:, :, :, lanes].astype(F32).reshape(owners // 2, 2, 16, ANGLES)
            upper = 8 * (quarter // 2)
            even = raw[:, 0, upper : upper + 8]
            odd = raw[:, 1, upper : upper + 8]
            if quarter % 2 == 0:
                rows = jnp.where(sub_index < 4, even, pltpu.roll(odd, 4, 1))
            else:
                rows = jnp.where(sub_index < 4, pltpu.roll(even, 4, 1), odd)
            rows = rows.reshape(local, ANGLES)
            norm_acc[...] += rows * rows
            for fine in range(FINE):
                moved = rows if fine == 0 else pltpu.roll(rows, ANGLES - fine, 1)
                cls_roll[fine * local : (fine + 1) * local, pl.ds(at, ANGLES)] = moved.astype(BF16)
            return carry

        lax.fori_loop(0, quarter_cycles, roll_classes, 0)

    for quarter in range(QUARTERS):
        cols = slice(quarter * width, (quarter + 1) * width)
        classes = cls_roll[:, cols]
        eight = contract_last(classes, part_hi[:, cols]) + contract_last(classes, part_lo[:, cols])
        ninth = contract_last(classes, part_ninth[:, cols])
        if quarter == 0:
            score_a[...] = eight
            score_b[...] = ninth
        else:
            score_a[...] += eight
            score_b[...] += ninth

    beta_copy.wait_recv()
    half_norm = 0.5 * jnp.sum(norm_acc[...], axis=1, keepdims=True)
    half_norm = jnp.concatenate([half_norm] * FINE, axis=0)
    lane_a = lax.broadcasted_iota(jnp.int32, (1, 32 * COARSE), 1)
    lane_b = lax.broadcasted_iota(jnp.int32, (1, 2 * ninth_rows), 1)
    who_a = (lane_a // 8) % 4
    who_b = ((lane_b // 8) % 2) * 2 + lane_b % 2
    first_b = lane_b < ninth_rows

    def along(values, who):
        return jnp.where(
            who == 0, values[0], jnp.where(who == 1, values[1], jnp.where(who == 2, values[2], values[3]))
        )

    betas = [beta_all[p // 2, p % 2 : p % 2 + 1, 0:1] for p in range(4)]
    full_b = score_b[...]
    full_b = full_b + pltpu.roll(full_b, ninth_rows, 1)
    full_a = along(betas, who_a) * (score_a[...] - half_norm)
    full_b = along(betas, who_b) * (full_b - half_norm)
    top_a = jnp.max(full_a, axis=0, keepdims=True)
    top_b = jnp.max(full_b, axis=0, keepdims=True)
    low = jnp.float32(-jnp.inf)

    def pick_max(p):
        return jnp.maximum(
            jnp.max(jnp.where(who_a == p, top_a, low), axis=1, keepdims=True),
            jnp.max(jnp.where(who_b == p, top_b, low), axis=1, keepdims=True),
        )

    tops = [pick_max(p) for p in range(4)]
    raised_a = jnp.exp(full_a - along(tops, who_a))
    raised_b = jnp.exp(full_b - along(tops, who_b))
    score_a[...] = raised_a
    score_b[...] = raised_b
    total_a = jnp.sum(raised_a, axis=0, keepdims=True)
    total_b = jnp.sum(raised_b, axis=0, keepdims=True)

    def pick_sum(p):
        return jnp.sum(jnp.where(who_a == p, total_a, 0.0), axis=1, keepdims=True) + jnp.sum(
            jnp.where((who_b == p) & first_b, total_b, 0.0), axis=1, keepdims=True
        )

    parts = [pick_sum(p) for p in range(4)]
    for p in range(4):
        stats[0, p : p + 1, :] = jnp.broadcast_to(tops[p], (1, ANGLES))
        stats[0, p + 4 : p + 5, :] = jnp.broadcast_to(parts[p], (1, ANGLES))
    stat_copy = start(
        remote(
            stats.at[0],
            stats.at[1],
            pair_send_sem.at[1 + QUARTERS],
            pair_recv_sem.at[1 + QUARTERS],
            partner,
        )
    )
    stat_copy.wait_recv()
    factors = []
    for p in range(4):
        other_top = stats[1, p : p + 1, 0:1]
        other_part = stats[1, p + 4 : p + 5, 0:1]
        top = jnp.maximum(tops[p], other_top)
        mine = jnp.exp(tops[p] - top)
        factors.append(mine / (parts[p] * mine + other_part * jnp.exp(other_top - top)))
    final_a = score_a[...] * along(factors, who_a)
    final_b = score_b[...] * along(factors, who_b)
    weight_a[...] = final_a.astype(BF16)
    weight_b[...] = final_b.astype(BF16)
    lane_sum = jnp.where(first_b, final_b, 0.0)
    for piece in range(32 * COARSE // ANGLES):
        lane_sum = lane_sum + final_a[:, piece * ANGLES : (piece + 1) * ANGLES]
    mass = lane_sum[0:local]
    for fine in range(1, FINE):
        mass = mass + lane_sum[fine * local : (fine + 1) * local]
    mass = jnp.broadcast_to(jnp.sum(mass, axis=1, keepdims=True), (local, ANGLES))
    for step in range(xs):
        xm_send[step] = mass[step * block_rows : (step + 1) * block_rows]
    mass_copies = [
        start(
            remote(
                xm_send.at[step],
                xm_recv.at[step],
                xm_send_sem.at[step],
                xm_recv_sem.at[step],
                x_peer(xs - step),
            )
        )
        for step in range(1, xs)
    ]

    sum_tiles = polar // SUM_TILE

    def weigh(tile, store):
        cols = pl.ds(pl.multiple_of(tile * SUM_TILE, SUM_TILE), SUM_TILE)
        store[...] = (
            matmul(weight_a[...], part_hi[:, cols])
            + matmul(weight_a[...], part_lo[:, cols])
            + matmul(weight_b[...], part_ninth[:, cols])
        )

    def x_copy(step, tile):
        return remote(
            x_send.at[step, tile],
            x_recv.at[step, tile],
            x_send_sem.at[step, tile],
            x_recv_sem.at[step, tile],
            x_peer(xs - step),
        )

    def unroll(tile, store):
        for piece in range(SUM_TILE // ANGLES):
            lanes = slice(piece * ANGLES, (piece + 1) * ANGLES)
            total = store[0:local, lanes]
            for fine in range(1, FINE):
                total = total + pltpu.roll(store[fine * local : (fine + 1) * local, lanes], fine, 1)
            own_sum[tile, :, lanes] = total[0:block_rows]
            for step in range(1, xs):
                x_send[step, tile, :, lanes] = total[
                    step * block_rows : (step + 1) * block_rows
                ].astype(BF16)
        for step in range(1, xs):
            x_copy(step, tile).start()

    weigh(0, grid_a)

    def sum_pair(step, carry):
        tile = 2 * step
        weigh(tile + 1, grid_b)
        unroll(tile, grid_a)
        weigh(jnp.minimum(tile + 2, sum_tiles - 1), grid_a)
        unroll(tile + 1, grid_b)
        return carry

    lax.fori_loop(0, sum_tiles // 2, sum_pair, 0)

    mass = xm_send[0]
    for step in range(1, xs):
        mass_copies[step - 1].wait_recv()
        mass = mass + xm_recv[step]
    for part in range(ys):
        y_send[part, :, y_width : y_width + ANGLES] = mass
    for tile in range(sum_tiles):
        total = own_sum[tile]
        for step in range(1, xs):
            x_copy(step, tile).wait_recv()
            total = total + x_recv[step, tile].astype(F32)
        at = tile * SUM_TILE
        y_send[at // y_width, :, at % y_width : at % y_width + SUM_TILE] = total
    y_copies = [
        start(
            remote(
                y_send.at[(y + step) % ys],
                y_recv.at[step],
                y_send_sem.at[step],
                y_recv_sem.at[step],
                y_peer(step),
            )
        )
        for step in range(1, ys)
    ]
    total = y_send[y]
    for step in range(1, ys):
        y_copies[step - 1].wait_recv()
        total = total + y_recv[step]
    for high in range(zhs):
        rows = total[OWNED * high : OWNED * high + OWNED]
        for low_at in range(zls):
            z_send[high, low_at, :, 0:z_width] = rows[:, low_at * z_width : (low_at + 1) * z_width]
            z_send[high, low_at, :, z_width : z_width + ANGLES] = rows[:, y_width : y_width + ANGLES]
    z_copies = [
        start(
            remote(
                z_send.at[high, (zl + low_at) % zls],
                z_recv.at[high, low_at],
                z_send_sem.at[high, low_at],
                z_recv_sem.at[high, low_at],
                z_peer(zhs - high, low_at),
            )
        )
        for high in range(zhs)
        for low_at in range(zls)
        if high or low_at
    ]
    total = z_send[0, zl]
    slots = [(high, low_at) for high in range(zhs) for low_at in range(zls) if high or low_at]
    for copy, (high, low_at) in zip(z_copies, slots):
        copy.wait_recv()
        total = total + z_recv[high, low_at]
    mass_ref[...] = total[:, z_width : z_width + ANGLES]
    gathered[grp] = total[:, 0:z_width]
    g_copies = [
        start(
            remote(
                gathered.at[grp],
                gathered.at[grp],
                g_send_sem.at[step_y, step_l],
                g_recv_sem.at[step_y, step_l],
                g_peer(step_y, step_l),
            )
        )
        for step_y in range(ys)
        for step_l in range(zls)
        if step_y or step_l
    ]
    for copy in g_copies:
        copy.wait_recv()
    for part in range(ys * zls):
        sums_ref[:, part * z_width : (part + 1) * z_width] = gathered[part]

    for tile in range(sum_tiles):
        for step in range(1, xs):
            x_copy(step, tile).wait_send()
    for copy in waits:
        copy.wait_send()


def on_device(layout, particles, inv_noise, class_images, col_factor, row_factor, row_shifts, col_shifts):
    xs, ys, zhs, zls = layout
    side = particles.shape[1]
    polar = col_factor.shape[1]
    cycles = polar // ANGLES
    width = polar // QUARTERS
    local = OWNED * xs * zhs
    block_rows = OWNED * zhs
    y_width = polar // ys
    z_width = y_width // zls
    sum_tiles = polar // SUM_TILE
    eight = 32 * COARSE
    ninth = 2 * 16 * (COARSE // SUBS)
    vmem = pltpu.VMEM
    dma = pltpu.SemaphoreType.DMA
    scratch = [
        vmem((2 * SHIFTS * side, side), BF16),
        vmem((2 * SHIFTS * side, POLAR_TILE), F32),
        vmem((2 * SHIFTS * side, POLAR_TILE), F32),
        vmem((cycles, side + 16, ANGLES), F32),
        vmem((16, width), F32),
        vmem((xs, zhs, 16, width), BF16),
        vmem((2, QUARTERS, 24, width), F32),
        vmem((2, 8, ANGLES), F32),
        vmem((2, 8, ANGLES), F32),
        vmem((eight, polar), BF16),
        vmem((eight, polar), BF16),
        vmem((ninth, polar), BF16),
        vmem((FINE * local, polar), BF16),
        vmem((local, ANGLES), F32),
        vmem((FINE * local, eight), F32),
        vmem((FINE * local, ninth), F32),
        vmem((FINE * local, eight), BF16),
        vmem((FINE * local, ninth), BF16),
        vmem((FINE * local, SUM_TILE), F32),
        vmem((FINE * local, SUM_TILE), F32),
        vmem((sum_tiles, block_rows, SUM_TILE), F32),
        vmem((xs, sum_tiles, block_rows, SUM_TILE), BF16),
        vmem((xs, sum_tiles, block_rows, SUM_TILE), BF16),
        vmem((xs, block_rows, ANGLES), F32),
        vmem((xs, block_rows, ANGLES), F32),
        vmem((ys, block_rows, y_width + ANGLES), F32),
        vmem((ys, block_rows, y_width + ANGLES), F32),
        vmem((zhs, zls, OWNED, z_width + ANGLES), F32),
        vmem((zhs, zls, OWNED, z_width + ANGLES), F32),
        vmem((ys * zls, OWNED, z_width), F32),
        dma((2 + QUARTERS,)),
        dma((2 + QUARTERS,)),
        dma((zhs,)),
        dma((zhs,)),
        dma((xs, zhs)),
        dma((xs, zhs)),
        dma((xs, sum_tiles)),
        dma((xs, sum_tiles)),
        dma((xs,)),
        dma((xs,)),
        dma((ys,)),
        dma((ys,)),
        dma((zhs, zls)),
        dma((zhs, zls)),
        dma((ys, zls)),
        dma((ys, zls)),
    ]
    in_vmem = pl.BlockSpec(memory_space=pltpu.VMEM)
    in_smem = pl.BlockSpec(memory_space=pltpu.SMEM)
    sums, mass = pl.pallas_call(
        functools.partial(kernel, layout),
        out_shape=(
            jax.ShapeDtypeStruct((OWNED, polar), F32),
            jax.ShapeDtypeStruct((OWNED, ANGLES), F32),
        ),
        in_specs=[in_vmem, in_smem, in_vmem, in_vmem, in_vmem, in_smem, in_smem],
        out_specs=(in_vmem, in_vmem),
        scratch_shapes=scratch,
        compiler_params=pltpu.CompilerParams(
            collective_id=0, has_side_effects=True, vmem_limit_bytes=60 * 1024 * 1024
        ),
        name="em_iteration",
    )(particles, inv_noise, class_images, col_factor, row_factor, row_shifts, col_shifts)
    occupancy = mass[:, 0]
    return sums / jnp.maximum(occupancy, 1.0)[:, None], occupancy


def solution(mesh, layout=(4, 4, 4, 2)):
    placed = (
        P(("grp", "own"), None, None),
        P(("grp", "own")),
        P("own", None, None),
        P(),
        P(),
        P(),
        P(),
    )
    return jax.shard_map(
        functools.partial(on_device, layout),
        mesh=mesh,
        in_specs=placed,
        out_specs=(P("own", None), P("own")),
        check_vma=False,
    )
```

```python
import functools

import jax
import jax.numpy as jnp
from jax import lax
from jax.experimental import pallas as pl
from jax.experimental.pallas import tpu as pltpu
from jax.sharding import PartitionSpec as P

F32 = jnp.float32
BF16 = jnp.bfloat16
ANGLES = 128
SHIFTS = 3
FINE = 8
COARSE = ANGLES // FINE
OWNED = 4
SUBS = 4
QUARTERS = 4
POLAR_TILE = 256
SUM_TILE = 512
MESH = pl.DeviceIdType.MESH


def contract_last(left, right):
    return lax.dot_general(left, right, (((1,), (1,)), ((), ())), preferred_element_type=F32)


def matmul(left, right):
    return jnp.dot(left, right, preferred_element_type=F32)


def kernel(
    layout,
    part_hbm,
    noise_ref,
    cls_hbm,
    col_hbm,
    row_hbm,
    rs_ref,
    cs_ref,
    new_ref,
    mass_ref,
    part_ref,
    cls_ref,
    col_ref,
    row_ref,
    pics,
    spread_a,
    spread_b,
    rowp,
    cp_f32,
    cp_all,
    pp_all,
    beta_all,
    stats,
    part_hi,
    part_lo,
    part_ninth,
    cls_roll,
    norm_acc,
    score_a,
    score_b,
    weight_a,
    weight_b,
    grid_a,
    grid_b,
    own_sum,
    x_send,
    x_recv,
    xm_send,
    xm_recv,
    z_send,
    z_recv,
    gathered,
    load_sem,
    pair_send_sem,
    pair_recv_sem,
    cz_send_sem,
    cz_recv_sem,
    cx_send_sem,
    cx_recv_sem,
    x_send_sem,
    x_recv_sem,
    xm_send_sem,
    xm_recv_sem,
    z_send_sem,
    z_recv_sem,
    g_send_sem,
    g_recv_sem,
):
    xs, ys, zhs, zls = layout
    side = part_ref.shape[1]
    polar = col_ref.shape[1]
    cycles = polar // ANGLES
    width = polar // QUARTERS
    quarter_cycles = cycles // QUARTERS
    owners = xs * zhs
    local = OWNED * owners
    block_rows = OWNED * zhs
    y_width = polar // ys
    z_width = y_width // zls

    cls_load = pltpu.make_async_copy(cls_hbm, cls_ref, load_sem.at[0])
    part_load = pltpu.make_async_copy(part_hbm, part_ref, load_sem.at[1])
    cls_load.start()
    factor_loads = []
    for quarter in range(QUARTERS):
        cols = slice(quarter * width, (quarter + 1) * width)
        pair = [
            pltpu.make_async_copy(col_hbm.at[:, cols], col_ref.at[:, cols], load_sem.at[2 + 2 * quarter]),
            pltpu.make_async_copy(row_hbm.at[:, cols], row_ref.at[:, cols], load_sem.at[3 + 2 * quarter]),
        ]
        for copy in pair:
            copy.start()
        factor_loads.append(pair)
    part_load.start()

    grp = lax.axis_index("grp")
    own = lax.axis_index("own")
    zl = grp % zls
    y = grp // zls
    core = own % 2
    x = (own // 2) % xs
    zh = own // (2 * xs)

    def device(y_at, zl_at, zh_at, x_at, core_at):
        return {"grp": y_at * zls + zl_at, "own": (zh_at * xs + x_at) * 2 + core_at}

    partner = device(y, zl, zh, x, 1 - core)

    def x_peer(step):
        return device(y, zl, zh, (x + step) % xs, core)

    def plane_peer(back, ahead):
        return device((y + ahead) % ys, zl, zh, (x + xs - back) % xs, core)

    def z_peer(high, low):
        return device(y, (zl + low) % zls, (zh + high) % zhs, x, core)

    def g_peer(step_y, step_l):
        return device((y + step_y) % ys, (zl + step_l) % zls, zh, x, core)

    peers = [partner]
    peers += [
        plane_peer(back, ahead) for back in range(xs) for ahead in range(ys) if back or ahead
    ]
    peers += [z_peer(high, low) for high in range(zhs) for low in range(zls) if high or low]
    peers += [
        g_peer(step_y, step_l) for step_y in range(1, ys) for step_l in range(1, zls)
    ]
    barrier = pltpu.get_barrier_semaphore()
    for peer in peers:
        pl.semaphore_signal(barrier, inc=1, device_id=peer, device_id_type=MESH)

    def remote(src, dst, send_sem, recv_sem, peer):
        return pltpu.make_async_remote_copy(
            src_ref=src,
            dst_ref=dst,
            send_sem=send_sem,
            recv_sem=recv_sem,
            device_id=peer,
            device_id_type=MESH,
        )

    def class_spread(tile, store):
        store[0 : OWNED * side, :] = matmul(
            cls_ref[...].reshape(OWNED * side, side),
            col_ref[:, pl.ds(pl.multiple_of(tile * POLAR_TILE, POLAR_TILE), POLAR_TILE)],
        )

    def class_reduce(tile, quarter, store):
        for half in range(POLAR_TILE // ANGLES):
            at = pl.multiple_of(tile * POLAR_TILE + half * ANGLES, ANGLES)
            place = pl.multiple_of(at - quarter * width, ANGLES)
            lanes = slice(half * ANGLES, (half + 1) * ANGLES)
            totals = [jnp.zeros((8, ANGLES), F32)] * OWNED
            for block in range(side // 16):
                rows = row_ref[block * 16 : block * 16 + 16, pl.ds(at, ANGLES)].astype(F32)
                for sub in range(2):
                    for k in range(OWNED):
                        start = k * side + block * 16 + sub * 8
                        totals[k] = totals[k] + store[start : start + 8, lanes] * rows[sub * 8 : sub * 8 + 8]
            for k in range(OWNED):
                cp_f32[quarter * OWNED + k : quarter * OWNED + k + 1, pl.ds(place, ANGLES)] = jnp.sum(
                    totals[k], axis=0, keepdims=True
                )

    tiles_per_quarter = width // POLAR_TILE
    last_tile = polar // POLAR_TILE - 1
    cls_load.wait()
    for quarter in range(QUARTERS):
        for copy in factor_loads[quarter]:
            copy.wait()
        last_of_quarter = (quarter + 1) * tiles_per_quarter - 1
        class_spread(quarter * tiles_per_quarter, spread_a)

        def class_pair(step, carry):
            tile = quarter * tiles_per_quarter + 2 * step
            class_spread(tile + 1, spread_b)
            class_reduce(tile, quarter, spread_a)
            class_spread(jnp.minimum(tile + 2, last_of_quarter), spread_a)
            class_reduce(tile + 1, quarter, spread_b)
            return carry

        lax.fori_loop(0, tiles_per_quarter // 2, class_pair, 0)
    cp_all[0, 0] = cp_f32[...].astype(BF16)

    pl.semaphore_wait(barrier, len(peers))
    waits = []

    def start(copy):
        copy.start()
        waits.append(copy)
        return copy

    gather_z = [None] + [
        start(
            remote(
                cp_all.at[0, 0],
                cp_all.at[0, high],
                cz_send_sem.at[high],
                cz_recv_sem.at[high],
                z_peer(high, 0),
            )
        )
        for high in range(1, zhs)
    ]
    gather_x = {}

    def forward(high):
        if high:
            gather_z[high].wait_recv()
        for step in range(1, xs):
            gather_x[step, high] = start(
                remote(
                    cp_all.at[0, high],
                    cp_all.at[step, high],
                    cx_send_sem.at[step, high],
                    cx_recv_sem.at[step, high],
                    x_peer(step),
                )
            )

    forward(0)

    beta_rows = lax.broadcasted_iota(jnp.int32, (8, ANGLES), 0)
    beta_all[core] = jnp.where(beta_rows == 0, noise_ref[0], noise_ref[1])
    beta_copy = start(
        remote(
            beta_all.at[core], beta_all.at[core], pair_send_sem.at[0], pair_recv_sem.at[0], partner
        )
    )

    part_load.wait()
    from_col = lax.broadcasted_iota(jnp.int32, (side, side), 0)
    to_col = lax.broadcasted_iota(jnp.int32, (side, side), 1)
    for j in range(SHIFTS):
        mover = jnp.where(((to_col - cs_ref[j]) & (side - 1)) == from_col, 1.0, 0.0).astype(BF16)
        for n in range(2):
            start_row = (n * SHIFTS + j) * side
            pics[start_row : start_row + side, :] = matmul(part_ref[n], mover).astype(BF16)

    def extend(cycle, carry):
        at = pl.multiple_of(cycle * ANGLES, ANGLES)
        values = row_ref[:, pl.ds(at, ANGLES)].astype(F32)
        rowp[cycle, 8 : side + 8, :] = values
        rowp[cycle, 0:8, :] = values[side - 8 : side]
        rowp[cycle, side + 8 : side + 16, :] = values[0:8]
        return carry

    lax.fori_loop(0, cycles, extend, 0)

    offsets = [rs_ref[i] for i in range(SHIFTS)]

    def part_spread(tile, store):
        store[...] = matmul(
            pics[...],
            col_ref[:, pl.ds(pl.multiple_of(tile * POLAR_TILE, POLAR_TILE), POLAR_TILE)],
        )

    def part_reduce(tile, quarter, store):
        for half in range(POLAR_TILE // ANGLES):
            cycle = tile * (POLAR_TILE // ANGLES) + half
            place = pl.multiple_of((cycle - quarter * quarter_cycles) * ANGLES, ANGLES)
            lanes = slice(half * ANGLES, (half + 1) * ANGLES)
            totals = [jnp.zeros((8, ANGLES), F32)] * (2 * SHIFTS * SHIFTS)
            for block in range(side // 8):
                rows = [
                    rowp[cycle, pl.ds(8 + block * 8 + offsets[i], 8), :] for i in range(SHIFTS)
                ]
                for n in range(2):
                    for j in range(SHIFTS):
                        begin = (n * SHIFTS + j) * side + block * 8
                        value = store[begin : begin + 8, lanes]
                        for i in range(SHIFTS):
                            index = n * 9 + i * SHIFTS + j
                            totals[index] = totals[index] + value * rows[i]
            for n in range(2):
                for s in range(8):
                    pp_all[core, quarter, 8 * n + s : 8 * n + s + 1, pl.ds(place, ANGLES)] = jnp.sum(
                        totals[n * 9 + s], axis=0, keepdims=True
                    )
                ninth = jnp.broadcast_to(
                    jnp.sum(totals[n * 9 + 8], axis=0, keepdims=True), (8, ANGLES)
                )
                for sub in range(SUBS):
                    row = 16 + 2 * sub + n
                    moved = ninth if sub == 0 else pltpu.roll(ninth, sub * FINE, 1)
                    pp_all[core, quarter, row : row + 1, pl.ds(place, ANGLES)] = moved[0:1]

    pair_copies = []
    part_spread(0, spread_a)
    for quarter in range(QUARTERS):

        def part_pair(step, carry):
            tile = quarter * tiles_per_quarter + 2 * step
            part_spread(tile + 1, spread_b)
            part_reduce(tile, quarter, spread_a)
            part_spread(jnp.minimum(tile + 2, last_tile), spread_a)
            part_reduce(tile + 1, quarter, spread_b)
            return carry

        lax.fori_loop(0, tiles_per_quarter // 2, part_pair, 0)
        pair_copies.append(
            start(
                remote(
                    pp_all.at[core, quarter],
                    pp_all.at[core, quarter],
                    pair_send_sem.at[1 + quarter],
                    pair_recv_sem.at[1 + quarter],
                    partner,
                )
            )
        )
        if quarter == 2:
            for high in range(1, zhs):
                forward(high)

    def split_store(value, rows, at, high_ref, low_ref, low_rows):
        high = value.astype(BF16)
        high_ref[rows, pl.ds(at, ANGLES)] = high
        low_ref[low_rows, pl.ds(at, ANGLES)] = (value - high.astype(F32)).astype(BF16)

    ninth_rows = 16 * (COARSE // SUBS)
    for quarter in range(QUARTERS):
        pair_copies[quarter].wait_recv()

        def roll_particles(step, carry):
            lanes = pl.ds(pl.multiple_of(step * ANGLES, ANGLES), ANGLES)
            at = pl.multiple_of(quarter * width + step * ANGLES, ANGLES)
            first = pp_all[0, quarter, :, lanes]
            second = pp_all[1, quarter, :, lanes]
            eight = jnp.concatenate([first[0:16], second[0:16]], axis=0)
            ninth = jnp.concatenate([first[16:24], second[16:24]], axis=0)
            for coarse in range(COARSE):
                moved = eight if coarse == 0 else pltpu.roll(eight, coarse * FINE, 1)
                rows = slice(32 * coarse, 32 * coarse + 32)
                split_store(moved, rows, at, part_hi, part_lo, rows)
            for coarse in range(COARSE // SUBS):
                moved = ninth if coarse == 0 else pltpu.roll(ninth, coarse * FINE * SUBS, 1)
                rows = slice(16 * coarse, 16 * coarse + 16)
                low_rows = slice(ninth_rows + 16 * coarse, ninth_rows + 16 * coarse + 16)
                split_store(moved, rows, at, part_ninth, part_ninth, low_rows)
            return carry

        lax.fori_loop(0, quarter_cycles, roll_particles, 0, unroll=4)

    for step in range(1, xs):
        for high in range(zhs):
            gather_x[step, high].wait_recv()
    norm_acc[...] = jnp.zeros_like(norm_acc)
    sub_index = lax.broadcasted_iota(jnp.int32, (owners // 2, 8, ANGLES), 1)
    for quarter in range(QUARTERS):

        def roll_classes(step, carry):
            lanes = pl.ds(pl.multiple_of(step * ANGLES, ANGLES), ANGLES)
            at = pl.multiple_of(quarter * width + step * ANGLES, ANGLES)
            raw = cp_all[:, :, :, lanes].astype(F32).reshape(owners // 2, 2, 16, ANGLES)
            upper = 8 * (quarter // 2)
            even = raw[:, 0, upper : upper + 8]
            odd = raw[:, 1, upper : upper + 8]
            if quarter % 2 == 0:
                rows = jnp.where(sub_index < 4, even, pltpu.roll(odd, 4, 1))
            else:
                rows = jnp.where(sub_index < 4, pltpu.roll(even, 4, 1), odd)
            rows = rows.reshape(local, ANGLES)
            norm_acc[...] += rows * rows
            for fine in range(FINE):
                moved = rows if fine == 0 else pltpu.roll(rows, ANGLES - fine, 1)
                cls_roll[fine * local : (fine + 1) * local, pl.ds(at, ANGLES)] = moved.astype(BF16)
            return carry

        lax.fori_loop(0, quarter_cycles, roll_classes, 0, unroll=4)

    for quarter in range(QUARTERS):
        cols = slice(quarter * width, (quarter + 1) * width)
        classes = cls_roll[:, cols]
        eight = contract_last(classes, part_hi[:, cols]) + contract_last(classes, part_lo[:, cols])
        ninth = contract_last(classes, part_ninth[:, cols])
        if quarter == 0:
            score_a[...] = eight
            score_b[...] = ninth
        else:
            score_a[...] += eight
            score_b[...] += ninth

    beta_copy.wait_recv()
    half_norm = 0.5 * jnp.sum(norm_acc[...], axis=1, keepdims=True)
    half_norm = jnp.concatenate([half_norm] * FINE, axis=0)
    lane_a = lax.broadcasted_iota(jnp.int32, (1, 32 * COARSE), 1)
    lane_b = lax.broadcasted_iota(jnp.int32, (1, 2 * ninth_rows), 1)
    who_a = (lane_a // 8) % 4
    who_b = ((lane_b // 8) % 2) * 2 + lane_b % 2
    first_b = lane_b < ninth_rows

    def along(values, who):
        return jnp.where(
            who == 0, values[0], jnp.where(who == 1, values[1], jnp.where(who == 2, values[2], values[3]))
        )

    betas = [beta_all[p // 2, p % 2 : p % 2 + 1, 0:1] for p in range(4)]
    full_b = score_b[...]
    full_b = full_b + pltpu.roll(full_b, ninth_rows, 1)
    full_a = along(betas, who_a) * (score_a[...] - half_norm)
    full_b = along(betas, who_b) * (full_b - half_norm)
    top_a = jnp.max(full_a, axis=0, keepdims=True)
    top_b = jnp.max(full_b, axis=0, keepdims=True)
    low = jnp.float32(-jnp.inf)

    def pick_max(p):
        return jnp.maximum(
            jnp.max(jnp.where(who_a == p, top_a, low), axis=1, keepdims=True),
            jnp.max(jnp.where(who_b == p, top_b, low), axis=1, keepdims=True),
        )

    tops = [pick_max(p) for p in range(4)]
    raised_a = jnp.exp(full_a - along(tops, who_a))
    raised_b = jnp.exp(full_b - along(tops, who_b))
    score_a[...] = raised_a
    score_b[...] = raised_b
    total_a = jnp.sum(raised_a, axis=0, keepdims=True)
    total_b = jnp.sum(raised_b, axis=0, keepdims=True)

    def pick_sum(p):
        return jnp.sum(jnp.where(who_a == p, total_a, 0.0), axis=1, keepdims=True) + jnp.sum(
            jnp.where((who_b == p) & first_b, total_b, 0.0), axis=1, keepdims=True
        )

    parts = [pick_sum(p) for p in range(4)]
    for p in range(4):
        stats[0, p : p + 1, :] = jnp.broadcast_to(tops[p], (1, ANGLES))
        stats[0, p + 4 : p + 5, :] = jnp.broadcast_to(parts[p], (1, ANGLES))
    stat_copy = start(
        remote(
            stats.at[0],
            stats.at[1],
            pair_send_sem.at[1 + QUARTERS],
            pair_recv_sem.at[1 + QUARTERS],
            partner,
        )
    )
    stat_copy.wait_recv()
    factors = []
    for p in range(4):
        other_top = stats[1, p : p + 1, 0:1]
        other_part = stats[1, p + 4 : p + 5, 0:1]
        top = jnp.maximum(tops[p], other_top)
        mine = jnp.exp(tops[p] - top)
        factors.append(mine / (parts[p] * mine + other_part * jnp.exp(other_top - top)))
    final_a = score_a[...] * along(factors, who_a)
    final_b = score_b[...] * along(factors, who_b)
    weight_a[...] = final_a.astype(BF16)
    weight_b[...] = final_b.astype(BF16)
    lane_sum = jnp.where(first_b, final_b, 0.0)
    for piece in range(32 * COARSE // ANGLES):
        lane_sum = lane_sum + final_a[:, piece * ANGLES : (piece + 1) * ANGLES]
    mass = lane_sum[0:local]
    for fine in range(1, FINE):
        mass = mass + lane_sum[fine * local : (fine + 1) * local]
    mass = jnp.broadcast_to(jnp.sum(mass, axis=1, keepdims=True), (local, ANGLES))
    for step in range(xs):
        xm_send[step] = mass[step * block_rows : (step + 1) * block_rows]

    def ahead_of(turn):
        if ys == 4:
            return (2 + turn + (turn // 2) * (1 + 2 * (turn % 2))) % 4
        return ys - 1 - turn

    def plane_copy(back, turn, side_at):
        return remote(
            x_send.at[back, turn, side_at],
            x_recv.at[back, turn, side_at],
            x_send_sem.at[back, turn, side_at],
            x_recv_sem.at[back, turn, side_at],
            plane_peer(back, ahead_of(turn)),
        )

    plane = [(back, turn) for back in range(xs) for turn in range(ys) if back or turn != ys - 1]
    mass_copies = [
        start(
            remote(
                xm_send.at[back],
                xm_recv.at[back, turn],
                xm_send_sem.at[back, turn],
                xm_recv_sem.at[back, turn],
                plane_peer(back, ahead_of(turn)),
            )
        )
        for back, turn in plane
    ]

    def weigh(tile, store):
        cols = pl.ds(pl.multiple_of(tile * SUM_TILE, SUM_TILE), SUM_TILE)
        store[...] = matmul(weight_a[...], part_hi[:, cols]) + matmul(
            weight_b[...], part_ninth[:, cols]
        )

    def unroll(turn, side_at, first, store):
        for piece in range(SUM_TILE // ANGLES):
            lanes = slice(piece * ANGLES, (piece + 1) * ANGLES)
            total = store[0:local, lanes]
            for fine in range(1, FINE):
                total = total + pltpu.roll(store[fine * local : (fine + 1) * local, lanes], fine, 1)
            if first:
                own_sum[side_at, :, lanes] = total[0:block_rows]
            for back in range(first, xs):
                x_send[back, turn, side_at, :, lanes] = total[
                    back * block_rows : (back + 1) * block_rows
                ].astype(BF16)
        for back in range(first, xs):
            plane_copy(back, turn, side_at).start()

    def tile_of(turn):
        return 2 * ((y + ahead_of(turn)) % ys)

    weigh(tile_of(0), grid_a)

    def sum_pair(turn, carry):
        weigh(tile_of(turn) + 1, grid_b)
        unroll(turn, 0, 0, grid_a)
        weigh(tile_of(turn + 1), grid_a)
        unroll(turn, 1, 0, grid_b)
        return carry

    lax.fori_loop(0, ys - 1, sum_pair, 0)
    weigh(2 * y + 1, grid_b)
    unroll(ys - 1, 0, 1, grid_a)
    unroll(ys - 1, 1, 1, grid_b)

    mass = xm_send[0]
    for copy, (back, turn) in zip(mass_copies, plane):
        copy.wait_recv()
        mass = mass + xm_recv[back, turn]
    halves = []
    for side_at in range(2):
        total = own_sum[side_at]
        for turn in range(ys):
            for back in range(xs):
                if back or turn != ys - 1:
                    plane_copy(back, turn, side_at).wait_recv()
                    total = total + x_recv[back, turn, side_at].astype(F32)
        halves.append(total)
    total = jnp.concatenate(halves + [mass], axis=1)
    for high in range(zhs):
        rows = total[OWNED * high : OWNED * high + OWNED]
        for low_at in range(zls):
            z_send[high, low_at, :, 0:z_width] = rows[:, low_at * z_width : (low_at + 1) * z_width]
            z_send[high, low_at, :, z_width : z_width + ANGLES] = rows[:, y_width : y_width + ANGLES]
    z_copies = [
        start(
            remote(
                z_send.at[high, (zl + low_at) % zls],
                z_recv.at[high, low_at],
                z_send_sem.at[high, low_at],
                z_recv_sem.at[high, low_at],
                z_peer(zhs - high, low_at),
            )
        )
        for high in range(zhs)
        for low_at in range(zls)
        if high or low_at
    ]
    total = z_send[0, zl]
    slots = [(high, low_at) for high in range(zhs) for low_at in range(zls) if high or low_at]
    for copy, (high, low_at) in zip(z_copies, slots):
        copy.wait_recv()
        total = total + z_recv[high, low_at]
    mass = total[:, z_width : z_width + ANGLES]
    on_diagonal = lax.broadcasted_iota(jnp.int32, (OWNED, ANGLES), 0) == lax.broadcasted_iota(
        jnp.int32, (OWNED, ANGLES), 1
    )
    mass_ref[...] = jnp.sum(jnp.where(on_diagonal, mass, 0.0), axis=0, keepdims=True)[:, 0:OWNED]
    gathered[grp] = total[:, 0:z_width] / jnp.maximum(mass[:, 0:1], 1.0)
    g_copies = [
        start(
            remote(
                gathered.at[grp],
                gathered.at[grp],
                g_send_sem.at[step_y, step_l],
                g_recv_sem.at[step_y, step_l],
                g_peer(step_y, step_l),
            )
        )
        for step_y in range(ys)
        for step_l in range(zls)
        if step_y or step_l
    ]
    for turn in range(ys):
        for back in range(xs):
            if back or turn != ys - 1:
                for side_at in range(2):
                    plane_copy(back, turn, side_at).wait_send()
    for copy in g_copies:
        copy.wait_recv()
    for part in range(ys * zls):
        new_ref[:, part * z_width : (part + 1) * z_width] = gathered[part]
    for copy in waits:
        copy.wait_send()


def on_device(layout, particles, inv_noise, class_images, col_factor, row_factor, row_shifts, col_shifts):
    xs, ys, zhs, zls = layout
    side = particles.shape[1]
    polar = col_factor.shape[1]
    cycles = polar // ANGLES
    width = polar // QUARTERS
    local = OWNED * xs * zhs
    block_rows = OWNED * zhs
    y_width = polar // ys
    z_width = y_width // zls
    eight = 32 * COARSE
    ninth = 2 * 16 * (COARSE // SUBS)
    vmem = pltpu.VMEM
    dma = pltpu.SemaphoreType.DMA
    scratch = [
        vmem((2, side, side), BF16),
        vmem((OWNED, side, side), BF16),
        vmem((side, polar), BF16),
        vmem((side, polar), BF16),
        vmem((2 * SHIFTS * side, side), BF16),
        vmem((2 * SHIFTS * side, POLAR_TILE), F32),
        vmem((2 * SHIFTS * side, POLAR_TILE), F32),
        vmem((cycles, side + 16, ANGLES), F32),
        vmem((16, width), F32),
        vmem((xs, zhs, 16, width), BF16),
        vmem((2, QUARTERS, 24, width), F32),
        vmem((2, 8, ANGLES), F32),
        vmem((2, 8, ANGLES), F32),
        vmem((eight, polar), BF16),
        vmem((eight, polar), BF16),
        vmem((ninth, polar), BF16),
        vmem((FINE * local, polar), BF16),
        vmem((local, ANGLES), F32),
        vmem((FINE * local, eight), F32),
        vmem((FINE * local, ninth), F32),
        vmem((FINE * local, eight), BF16),
        vmem((FINE * local, ninth), BF16),
        vmem((FINE * local, SUM_TILE), F32),
        vmem((FINE * local, SUM_TILE), F32),
        vmem((2, block_rows, SUM_TILE), F32),
        vmem((xs, ys, 2, block_rows, SUM_TILE), BF16),
        vmem((xs, ys, 2, block_rows, SUM_TILE), BF16),
        vmem((xs, block_rows, ANGLES), F32),
        vmem((xs, ys, block_rows, ANGLES), F32),
        vmem((zhs, zls, OWNED, z_width + ANGLES), F32),
        vmem((zhs, zls, OWNED, z_width + ANGLES), F32),
        vmem((ys * zls, OWNED, z_width), F32),
        dma((2 + 2 * QUARTERS,)),
        dma((2 + QUARTERS,)),
        dma((2 + QUARTERS,)),
        dma((zhs,)),
        dma((zhs,)),
        dma((xs, zhs)),
        dma((xs, zhs)),
        dma((xs, ys, 2)),
        dma((xs, ys, 2)),
        dma((xs, ys)),
        dma((xs, ys)),
        dma((zhs, zls)),
        dma((zhs, zls)),
        dma((ys, zls)),
        dma((ys, zls)),
    ]
    in_vmem = pl.BlockSpec(memory_space=pltpu.VMEM)
    in_smem = pl.BlockSpec(memory_space=pltpu.SMEM)
    in_hbm = pl.BlockSpec(memory_space=pl.ANY)
    new_averages, occupancy = pl.pallas_call(
        functools.partial(kernel, layout),
        out_shape=(
            jax.ShapeDtypeStruct((OWNED, polar), F32),
            jax.ShapeDtypeStruct((1, OWNED), F32),
        ),
        in_specs=[in_hbm, in_smem, in_hbm, in_hbm, in_hbm, in_smem, in_smem],
        out_specs=(in_vmem, in_vmem),
        scratch_shapes=scratch,
        compiler_params=pltpu.CompilerParams(
            collective_id=0, has_side_effects=True, vmem_limit_bytes=60 * 1024 * 1024
        ),
        name="em_iteration",
    )(particles, inv_noise, class_images, col_factor, row_factor, row_shifts, col_shifts)
    return new_averages, occupancy.reshape(OWNED)


def solution(mesh, layout=(4, 4, 4, 2)):
    placed = (
        P(("grp", "own"), None, None),
        P(("grp", "own")),
        P("own", None, None),
        P(),
        P(),
        P(),
        P(),
    )
    return jax.shard_map(
        functools.partial(on_device, layout),
        mesh=mesh,
        in_specs=placed,
        out_specs=(P("own", None), P("own")),
        check_vma=False,
    )
```

```python
import functools

import jax
import jax.numpy as jnp
from jax import lax
from jax.experimental import pallas as pl
from jax.experimental.pallas import tpu as pltpu
from jax.sharding import PartitionSpec as P

F32 = jnp.float32
BF16 = jnp.bfloat16
ANGLES = 128
SHIFTS = 3
FINE = 8
COARSE = ANGLES // FINE
OWNED = 4
SUBS = 4
QUARTERS = 4
POLAR_TILE = 256
CLASS_TILES = 4
SUM_TILE = 512
MESH = pl.DeviceIdType.MESH


def contract_last(left, right):
    return lax.dot_general(left, right, (((1,), (1,)), ((), ())), preferred_element_type=F32)


def matmul(left, right):
    return jnp.dot(left, right, preferred_element_type=F32)


def kernel(
    layout,
    part_hbm,
    noise_ref,
    cls_hbm,
    col_hbm,
    row_hbm,
    rs_ref,
    cs_ref,
    new_ref,
    mass_ref,
    part_ref,
    cls_ref,
    col_ref,
    row_ref,
    pics,
    spread_a,
    spread_b,
    rowp,
    cp_f32,
    cp_block,
    cp_wide,
    cp_all,
    pp_all,
    beta_all,
    stats,
    part_hi,
    part_lo,
    part_ninth,
    cls_roll,
    norm_acc,
    score_a,
    score_b,
    weight_a,
    weight_b,
    grid_a,
    grid_b,
    own_sum,
    x_send,
    x_recv,
    xm_send,
    xm_recv,
    z_send,
    z_recv,
    gathered,
    load_sem,
    pair_send_sem,
    pair_recv_sem,
    cz_send_sem,
    cz_recv_sem,
    cx_send_sem,
    cx_recv_sem,
    x_send_sem,
    x_recv_sem,
    xm_send_sem,
    xm_recv_sem,
    z_send_sem,
    z_recv_sem,
    g_send_sem,
    g_recv_sem,
):
    xs, ys, zhs, zls = layout
    side = part_ref.shape[1]
    polar = col_ref.shape[1]
    cycles = polar // ANGLES
    width = polar // QUARTERS
    quarter_cycles = cycles // QUARTERS
    owners = xs * zhs
    local = OWNED * owners
    block_rows = OWNED * zhs
    y_width = polar // ys
    z_width = y_width // zls

    grp = lax.axis_index("grp")
    own = lax.axis_index("own")
    zl = grp % zls
    y = grp // zls
    core = own % 2
    x = (own // 2) % xs
    zh = own // (2 * xs)

    def chunk_at(turn):
        return pl.multiple_of(((y + turn) % ys) * y_width, y_width)

    cls_load = pltpu.make_async_copy(cls_hbm, cls_ref, load_sem.at[0])
    part_load = pltpu.make_async_copy(part_hbm, part_ref, load_sem.at[1])
    cls_load.start()
    factor_loads = []
    for turn in range(ys):
        cols = pl.ds(chunk_at(turn), y_width)
        pair = [
            pltpu.make_async_copy(col_hbm.at[:, cols], col_ref.at[:, cols], load_sem.at[2 + 2 * turn]),
            pltpu.make_async_copy(row_hbm.at[:, cols], row_ref.at[:, cols], load_sem.at[3 + 2 * turn]),
        ]
        for copy in pair:
            copy.start()
        factor_loads.append(pair)
        if turn == 0:
            part_load.start()

    def device(y_at, zl_at, zh_at, x_at, core_at):
        return {"grp": y_at * zls + zl_at, "own": (zh_at * xs + x_at) * 2 + core_at}

    partner = device(y, zl, zh, x, 1 - core)

    def x_peer(step):
        return device(y, zl, zh, (x + step) % xs, core)

    def plane_peer(back, ahead):
        return device((y + ahead) % ys, zl, zh, (x + xs - back) % xs, core)

    def z_peer(high, low):
        return device(y, (zl + low) % zls, (zh + high) % zhs, x, core)

    def g_peer(step_y, step_l):
        return device((y + step_y) % ys, (zl + step_l) % zls, zh, x, core)

    peers = [partner]
    peers += [
        plane_peer(back, ahead) for back in range(xs) for ahead in range(ys) if back or ahead
    ]
    peers += [z_peer(high, low) for high in range(zhs) for low in range(zls) if high or low]
    peers += [
        g_peer(step_y, step_l) for step_y in range(1, ys) for step_l in range(1, zls)
    ]
    barrier = pltpu.get_barrier_semaphore()
    for peer in peers:
        pl.semaphore_signal(barrier, inc=1, device_id=peer, device_id_type=MESH)

    def remote(src, dst, send_sem, recv_sem, peer):
        return pltpu.make_async_remote_copy(
            src_ref=src,
            dst_ref=dst,
            send_sem=send_sem,
            recv_sem=recv_sem,
            device_id=peer,
            device_id_type=MESH,
        )

    def class_spread(tile, store):
        store[0 : OWNED * side, :] = matmul(
            cls_ref[...].reshape(OWNED * side, side),
            col_ref[:, pl.ds(pl.multiple_of(y * y_width + tile * POLAR_TILE, POLAR_TILE), POLAR_TILE)],
        )

    def class_reduce(tile, store):
        for half in range(POLAR_TILE // ANGLES):
            at = pl.multiple_of(y * y_width + tile * POLAR_TILE + half * ANGLES, ANGLES)
            lanes = slice(half * ANGLES, (half + 1) * ANGLES)
            totals = [jnp.zeros((8, ANGLES), F32)] * OWNED
            for block in range(side // 16):
                rows = row_ref[block * 16 : block * 16 + 16, pl.ds(at, ANGLES)].astype(F32)
                for sub in range(2):
                    for k in range(OWNED):
                        start = k * side + block * 16 + sub * 8
                        totals[k] = totals[k] + store[start : start + 8, lanes] * rows[sub * 8 : sub * 8 + 8]
            for k in range(OWNED):
                cp_f32[tile * OWNED + k : tile * OWNED + k + 1, lanes] = jnp.sum(
                    totals[k], axis=0, keepdims=True
                )

    tiles_per_quarter = width // POLAR_TILE
    last_tile = polar // POLAR_TILE - 1
    cls_load.wait()
    for copy in factor_loads[0]:
        copy.wait()
    spreads = [spread_a, spread_b]
    class_spread(0, spread_a)
    for tile in range(CLASS_TILES):
        if tile + 1 < CLASS_TILES:
            class_spread(tile + 1, spreads[(tile + 1) % 2])
        class_reduce(tile, spreads[tile % 2])
    cp_block[0] = cp_f32[...].astype(BF16)

    pl.semaphore_wait(barrier, len(peers))
    waits = []

    def start(copy):
        copy.start()
        waits.append(copy)
        return copy

    gather_z = [
        start(
            remote(
                cp_block.at[0],
                cp_block.at[high],
                cz_send_sem.at[high],
                cz_recv_sem.at[high],
                z_peer(high, 0),
            )
        )
        for high in range(1, zhs)
    ]
    gather = {}

    def forward():
        for copy in gather_z:
            copy.wait_recv()
        for high in range(zhs):
            block = cp_block[high].astype(F32)
            for tile in range(CLASS_TILES):
                cp_wide[
                    OWNED * high : OWNED * high + OWNED, tile * POLAR_TILE : (tile + 1) * POLAR_TILE
                ] = block[OWNED * tile : OWNED * tile + OWNED]
        cp_all[0, 0] = cp_wide[...].astype(BF16)
        for turn in range(ys):
            for step in range(xs):
                if step or turn:
                    gather[step, turn] = start(
                        remote(
                            cp_all.at[0, 0],
                            cp_all.at[step, turn],
                            cx_send_sem.at[step, turn],
                            cx_recv_sem.at[step, turn],
                            plane_peer(xs - step, ys - turn),
                        )
                    )

    beta_rows = lax.broadcasted_iota(jnp.int32, (8, ANGLES), 0)
    beta_all[core] = jnp.where(beta_rows == 0, noise_ref[0], noise_ref[1])
    beta_copy = start(
        remote(
            beta_all.at[core], beta_all.at[core], pair_send_sem.at[0], pair_recv_sem.at[0], partner
        )
    )

    for pair in factor_loads[1:]:
        for copy in pair:
            copy.wait()
    part_load.wait()
    from_col = lax.broadcasted_iota(jnp.int32, (side, side), 0)
    to_col = lax.broadcasted_iota(jnp.int32, (side, side), 1)
    for j in range(SHIFTS):
        mover = jnp.where(((to_col - cs_ref[j]) & (side - 1)) == from_col, 1.0, 0.0).astype(BF16)
        for n in range(2):
            start_row = (n * SHIFTS + j) * side
            pics[start_row : start_row + side, :] = matmul(part_ref[n], mover).astype(BF16)

    def extend(cycle, carry):
        at = pl.multiple_of(cycle * ANGLES, ANGLES)
        values = row_ref[:, pl.ds(at, ANGLES)].astype(F32)
        rowp[cycle, 8 : side + 8, :] = values
        rowp[cycle, 0:8, :] = values[side - 8 : side]
        rowp[cycle, side + 8 : side + 16, :] = values[0:8]
        return carry

    lax.fori_loop(0, cycles, extend, 0)

    offsets = [rs_ref[i] for i in range(SHIFTS)]

    def part_spread(tile, store):
        store[...] = matmul(
            pics[...],
            col_ref[:, pl.ds(pl.multiple_of(tile * POLAR_TILE, POLAR_TILE), POLAR_TILE)],
        )

    def part_reduce(tile, quarter, store):
        for half in range(POLAR_TILE // ANGLES):
            cycle = tile * (POLAR_TILE // ANGLES) + half
            place = pl.multiple_of((cycle - quarter * quarter_cycles) * ANGLES, ANGLES)
            lanes = slice(half * ANGLES, (half + 1) * ANGLES)
            totals = [jnp.zeros((8, ANGLES), F32)] * (2 * SHIFTS * SHIFTS)
            for block in range(side // 8):
                rows = [
                    rowp[cycle, pl.ds(8 + block * 8 + offsets[i], 8), :] for i in range(SHIFTS)
                ]
                for n in range(2):
                    for j in range(SHIFTS):
                        begin = (n * SHIFTS + j) * side + block * 8
                        value = store[begin : begin + 8, lanes]
                        for i in range(SHIFTS):
                            index = n * 9 + i * SHIFTS + j
                            totals[index] = totals[index] + value * rows[i]
            for n in range(2):
                for s in range(8):
                    pp_all[core, quarter, 8 * n + s : 8 * n + s + 1, pl.ds(place, ANGLES)] = jnp.sum(
                        totals[n * 9 + s], axis=0, keepdims=True
                    )
                ninth = jnp.broadcast_to(
                    jnp.sum(totals[n * 9 + 8], axis=0, keepdims=True), (8, ANGLES)
                )
                for sub in range(SUBS):
                    row = 16 + 2 * sub + n
                    moved = ninth if sub == 0 else pltpu.roll(ninth, sub * FINE, 1)
                    pp_all[core, quarter, row : row + 1, pl.ds(place, ANGLES)] = moved[0:1]

    pair_copies = []
    part_spread(0, spread_a)
    for quarter in range(QUARTERS):

        def part_pair(step, carry):
            tile = quarter * tiles_per_quarter + 2 * step
            part_spread(tile + 1, spread_b)
            part_reduce(tile, quarter, spread_a)
            part_spread(jnp.minimum(tile + 2, last_tile), spread_a)
            part_reduce(tile + 1, quarter, spread_b)
            return carry

        lax.fori_loop(0, tiles_per_quarter // 2, part_pair, 0)
        pair_copies.append(
            start(
                remote(
                    pp_all.at[core, quarter],
                    pp_all.at[core, quarter],
                    pair_send_sem.at[1 + quarter],
                    pair_recv_sem.at[1 + quarter],
                    partner,
                )
            )
        )
        if quarter == 1:
            forward()

    def split_store(value, rows, at, high_ref, low_ref, low_rows):
        high = value.astype(BF16)
        high_ref[rows, pl.ds(at, ANGLES)] = high
        low_ref[low_rows, pl.ds(at, ANGLES)] = (value - high.astype(F32)).astype(BF16)

    ninth_rows = 16 * (COARSE // SUBS)
    for quarter in range(QUARTERS):
        pair_copies[quarter].wait_recv()

        def roll_particles(step, carry):
            lanes = pl.ds(pl.multiple_of(step * ANGLES, ANGLES), ANGLES)
            at = pl.multiple_of(quarter * width + step * ANGLES, ANGLES)
            first = pp_all[0, quarter, :, lanes]
            second = pp_all[1, quarter, :, lanes]
            eight = jnp.concatenate([first[0:16], second[0:16]], axis=0)
            ninth = jnp.concatenate([first[16:24], second[16:24]], axis=0)
            for coarse in range(COARSE):
                moved = eight if coarse == 0 else pltpu.roll(eight, coarse * FINE, 1)
                rows = slice(32 * coarse, 32 * coarse + 32)
                split_store(moved, rows, at, part_hi, part_lo, rows)
            for coarse in range(COARSE // SUBS):
                moved = ninth if coarse == 0 else pltpu.roll(ninth, coarse * FINE * SUBS, 1)
                rows = slice(16 * coarse, 16 * coarse + 16)
                low_rows = slice(ninth_rows + 16 * coarse, ninth_rows + 16 * coarse + 16)
                split_store(moved, rows, at, part_ninth, part_ninth, low_rows)
            return carry

        lax.fori_loop(0, quarter_cycles, roll_particles, 0, unroll=4)

    norm_acc[...] = jnp.zeros_like(norm_acc)

    def roll_classes(turn):
        for step in range(xs):
            if step or turn:
                gather[step, turn].wait_recv()
        norm = norm_acc[...]
        for cycle in range(y_width // ANGLES):
            lanes = slice(cycle * ANGLES, (cycle + 1) * ANGLES)
            at = slice(turn * y_width + cycle * ANGLES, turn * y_width + (cycle + 1) * ANGLES)
            rows = cp_all[:, turn, :, lanes].astype(F32).reshape(local, ANGLES)
            norm = norm + rows * rows
            for fine in range(FINE):
                moved = rows if fine == 0 else pltpu.roll(rows, ANGLES - fine, 1)
                cls_roll[fine * local : (fine + 1) * local, at] = moved.astype(BF16)
        norm_acc[...] = norm

    roll_classes(0)
    for turn in range(ys):
        if turn + 1 < ys:
            roll_classes(turn + 1)
        classes = cls_roll[:, turn * y_width : (turn + 1) * y_width]
        cols = pl.ds(chunk_at(turn), y_width)
        eight = contract_last(classes, part_hi[:, cols]) + contract_last(classes, part_lo[:, cols])
        ninth = contract_last(classes, part_ninth[:, cols])
        if turn == 0:
            score_a[...] = eight
            score_b[...] = ninth
        else:
            score_a[...] += eight
            score_b[...] += ninth

    beta_copy.wait_recv()
    half_norm = 0.5 * jnp.sum(norm_acc[...], axis=1, keepdims=True)
    half_norm = jnp.concatenate([half_norm] * FINE, axis=0)
    lane_a = lax.broadcasted_iota(jnp.int32, (1, 32 * COARSE), 1)
    lane_b = lax.broadcasted_iota(jnp.int32, (1, 2 * ninth_rows), 1)
    who_a = (lane_a // 8) % 4
    who_b = ((lane_b // 8) % 2) * 2 + lane_b % 2
    first_b = lane_b < ninth_rows

    def along(values, who):
        return jnp.where(
            who == 0, values[0], jnp.where(who == 1, values[1], jnp.where(who == 2, values[2], values[3]))
        )

    betas = [beta_all[p // 2, p % 2 : p % 2 + 1, 0:1] for p in range(4)]
    full_b = score_b[...]
    full_b = full_b + pltpu.roll(full_b, ninth_rows, 1)
    full_a = along(betas, who_a) * (score_a[...] - half_norm)
    full_b = along(betas, who_b) * (full_b - half_norm)
    top_a = jnp.max(full_a, axis=0, keepdims=True)
    top_b = jnp.max(full_b, axis=0, keepdims=True)
    low = jnp.float32(-jnp.inf)

    def pick_max(p):
        return jnp.maximum(
            jnp.max(jnp.where(who_a == p, top_a, low), axis=1, keepdims=True),
            jnp.max(jnp.where(who_b == p, top_b, low), axis=1, keepdims=True),
        )

    tops = [pick_max(p) for p in range(4)]
    raised_a = jnp.exp(full_a - along(tops, who_a))
    raised_b = jnp.exp(full_b - along(tops, who_b))
    score_a[...] = raised_a
    score_b[...] = raised_b
    total_a = jnp.sum(raised_a, axis=0, keepdims=True)
    total_b = jnp.sum(raised_b, axis=0, keepdims=True)

    def pick_sum(p):
        return jnp.sum(jnp.where(who_a == p, total_a, 0.0), axis=1, keepdims=True) + jnp.sum(
            jnp.where((who_b == p) & first_b, total_b, 0.0), axis=1, keepdims=True
        )

    parts = [pick_sum(p) for p in range(4)]
    for p in range(4):
        stats[0, p : p + 1, :] = jnp.broadcast_to(tops[p], (1, ANGLES))
        stats[0, p + 4 : p + 5, :] = jnp.broadcast_to(parts[p], (1, ANGLES))
    stat_copy = start(
        remote(
            stats.at[0],
            stats.at[1],
            pair_send_sem.at[1 + QUARTERS],
            pair_recv_sem.at[1 + QUARTERS],
            partner,
        )
    )
    stat_copy.wait_recv()
    factors = []
    for p in range(4):
        other_top = stats[1, p : p + 1, 0:1]
        other_part = stats[1, p + 4 : p + 5, 0:1]
        top = jnp.maximum(tops[p], other_top)
        mine = jnp.exp(tops[p] - top)
        factors.append(mine / (parts[p] * mine + other_part * jnp.exp(other_top - top)))
    final_a = score_a[...] * along(factors, who_a)
    final_b = score_b[...] * along(factors, who_b)
    weight_a[...] = final_a.astype(BF16)
    weight_b[...] = final_b.astype(BF16)
    lane_sum = jnp.where(first_b, final_b, 0.0)
    for piece in range(32 * COARSE // ANGLES):
        lane_sum = lane_sum + final_a[:, piece * ANGLES : (piece + 1) * ANGLES]
    mass = lane_sum[0:local]
    for fine in range(1, FINE):
        mass = mass + lane_sum[fine * local : (fine + 1) * local]
    mass = jnp.broadcast_to(jnp.sum(mass, axis=1, keepdims=True), (local, ANGLES))
    for step in range(xs):
        xm_send[step] = mass[step * block_rows : (step + 1) * block_rows]

    def ahead_of(turn):
        if ys == 4:
            return (2 + turn + (turn // 2) * (1 + 2 * (turn % 2))) % 4
        return ys - 1 - turn

    def plane_copy(back, turn, side_at):
        return remote(
            x_send.at[back, turn, side_at],
            x_recv.at[back, turn, side_at],
            x_send_sem.at[back, turn, side_at],
            x_recv_sem.at[back, turn, side_at],
            plane_peer(back, ahead_of(turn)),
        )

    mass_copies = [
        start(
            remote(
                xm_send.at[back],
                xm_recv.at[back],
                xm_send_sem.at[back],
                xm_recv_sem.at[back],
                plane_peer(back, 0),
            )
        )
        for back in range(1, xs)
    ]

    def weigh(tile, store):
        cols = pl.ds(pl.multiple_of(tile * SUM_TILE, SUM_TILE), SUM_TILE)
        store[...] = matmul(weight_a[...], part_hi[:, cols]) + matmul(
            weight_b[...], part_ninth[:, cols]
        )

    def unroll(turn, side_at, first, store):
        for piece in range(SUM_TILE // ANGLES):
            lanes = slice(piece * ANGLES, (piece + 1) * ANGLES)
            total = store[0:local, lanes]
            for fine in range(1, FINE):
                total = total + pltpu.roll(store[fine * local : (fine + 1) * local, lanes], fine, 1)
            if first:
                own_sum[side_at, :, lanes] = total[0:block_rows]
            for back in range(first, xs):
                x_send[back, turn, side_at, :, lanes] = total[
                    back * block_rows : (back + 1) * block_rows
                ].astype(BF16)
        for back in range(first, xs):
            plane_copy(back, turn, side_at).start()

    def tile_of(turn):
        return 2 * ((y + ahead_of(turn)) % ys)

    weigh(tile_of(0), grid_a)

    def sum_pair(turn, carry):
        weigh(tile_of(turn) + 1, grid_b)
        unroll(turn, 0, 0, grid_a)
        weigh(tile_of(turn + 1), grid_a)
        unroll(turn, 1, 0, grid_b)
        return carry

    lax.fori_loop(0, ys - 1, sum_pair, 0)
    weigh(2 * y + 1, grid_b)
    unroll(ys - 1, 0, 1, grid_a)
    unroll(ys - 1, 1, 1, grid_b)

    mass = xm_send[0]
    for back in range(1, xs):
        mass_copies[back - 1].wait_recv()
        mass = mass + xm_recv[back]
    halves = []
    for side_at in range(2):
        total = own_sum[side_at]
        for turn in range(ys):
            for back in range(xs):
                if back or turn != ys - 1:
                    plane_copy(back, turn, side_at).wait_recv()
                    total = total + x_recv[back, turn, side_at].astype(F32)
        halves.append(total)
    total = jnp.concatenate(halves + [mass], axis=1)
    for high in range(zhs):
        rows = total[OWNED * high : OWNED * high + OWNED]
        for low_at in range(zls):
            z_send[high, low_at, :, 0:z_width] = rows[:, low_at * z_width : (low_at + 1) * z_width]
            z_send[high, low_at, :, z_width : z_width + ANGLES] = rows[:, y_width : y_width + ANGLES]
    z_copies = [
        start(
            remote(
                z_send.at[high, (zl + low_at) % zls],
                z_recv.at[high, low_at],
                z_send_sem.at[high, low_at],
                z_recv_sem.at[high, low_at],
                z_peer(zhs - high, low_at),
            )
        )
        for high in range(zhs)
        for low_at in range(zls)
        if high or low_at
    ]
    total = z_send[0, zl]
    slots = [(high, low_at) for high in range(zhs) for low_at in range(zls) if high or low_at]
    for copy, (high, low_at) in zip(z_copies, slots):
        copy.wait_recv()
        total = total + z_recv[high, low_at]
    gathered[grp] = total
    g_copies = [
        start(
            remote(
                gathered.at[grp],
                gathered.at[grp],
                g_send_sem.at[step_y, step_l],
                g_recv_sem.at[step_y, step_l],
                g_peer(step_y, step_l),
            )
        )
        for step_y in range(ys)
        for step_l in range(zls)
        if step_y or step_l
    ]
    for turn in range(ys):
        for back in range(xs):
            if back or turn != ys - 1:
                for side_at in range(2):
                    plane_copy(back, turn, side_at).wait_send()
    for copy in g_copies:
        copy.wait_recv()
    mass = gathered[0, :, z_width : z_width + ANGLES]
    for part in range(1, ys):
        mass = mass + gathered[part * zls, :, z_width : z_width + ANGLES]
    on_diagonal = lax.broadcasted_iota(jnp.int32, (OWNED, ANGLES), 0) == lax.broadcasted_iota(
        jnp.int32, (OWNED, ANGLES), 1
    )
    mass_ref[...] = jnp.sum(jnp.where(on_diagonal, mass, 0.0), axis=0, keepdims=True)[:, 0:OWNED]
    divisor = jnp.maximum(mass[:, 0:1], 1.0)
    for part in range(ys * zls):
        new_ref[:, part * z_width : (part + 1) * z_width] = gathered[part, :, 0:z_width] / divisor
    for copy in waits:
        copy.wait_send()


def on_device(layout, particles, inv_noise, class_images, col_factor, row_factor, row_shifts, col_shifts):
    xs, ys, zhs, zls = layout
    side = particles.shape[1]
    polar = col_factor.shape[1]
    cycles = polar // ANGLES
    width = polar // QUARTERS
    local = OWNED * xs * zhs
    block_rows = OWNED * zhs
    y_width = polar // ys
    z_width = y_width // zls
    eight = 32 * COARSE
    ninth = 2 * 16 * (COARSE // SUBS)
    vmem = pltpu.VMEM
    dma = pltpu.SemaphoreType.DMA
    scratch = [
        vmem((2, side, side), BF16),
        vmem((OWNED, side, side), BF16),
        vmem((side, polar), BF16),
        vmem((side, polar), BF16),
        vmem((2 * SHIFTS * side, side), BF16),
        vmem((2 * SHIFTS * side, POLAR_TILE), F32),
        vmem((2 * SHIFTS * side, POLAR_TILE), F32),
        vmem((cycles, side + 16, ANGLES), F32),
        vmem((OWNED * CLASS_TILES, POLAR_TILE), F32),
        vmem((zhs, OWNED * CLASS_TILES, POLAR_TILE), BF16),
        vmem((block_rows, y_width), F32),
        vmem((xs, ys, block_rows, y_width), BF16),
        vmem((2, QUARTERS, 24, width), F32),
        vmem((2, 8, ANGLES), F32),
        vmem((2, 8, ANGLES), F32),
        vmem((eight, polar), BF16),
        vmem((eight, polar), BF16),
        vmem((ninth, polar), BF16),
        vmem((FINE * local, polar), BF16),
        vmem((local, ANGLES), F32),
        vmem((FINE * local, eight), F32),
        vmem((FINE * local, ninth), F32),
        vmem((FINE * local, eight), BF16),
        vmem((FINE * local, ninth), BF16),
        vmem((FINE * local, SUM_TILE), F32),
        vmem((FINE * local, SUM_TILE), F32),
        vmem((2, block_rows, SUM_TILE), F32),
        vmem((xs, ys, 2, block_rows, SUM_TILE), BF16),
        vmem((xs, ys, 2, block_rows, SUM_TILE), BF16),
        vmem((xs, block_rows, ANGLES), F32),
        vmem((xs, block_rows, ANGLES), F32),
        vmem((zhs, zls, OWNED, z_width + ANGLES), F32),
        vmem((zhs, zls, OWNED, z_width + ANGLES), F32),
        vmem((ys * zls, OWNED, z_width + ANGLES), F32),
        dma((2 + 2 * ys,)),
        dma((2 + QUARTERS,)),
        dma((2 + QUARTERS,)),
        dma((zhs,)),
        dma((zhs,)),
        dma((xs, ys)),
        dma((xs, ys)),
        dma((xs, ys, 2)),
        dma((xs, ys, 2)),
        dma((xs,)),
        dma((xs,)),
        dma((zhs, zls)),
        dma((zhs, zls)),
        dma((ys, zls)),
        dma((ys, zls)),
    ]
    in_vmem = pl.BlockSpec(memory_space=pltpu.VMEM)
    in_smem = pl.BlockSpec(memory_space=pltpu.SMEM)
    in_hbm = pl.BlockSpec(memory_space=pl.ANY)
    new_averages, occupancy = pl.pallas_call(
        functools.partial(kernel, layout),
        out_shape=(
            jax.ShapeDtypeStruct((OWNED, polar), F32),
            jax.ShapeDtypeStruct((1, OWNED), F32),
        ),
        in_specs=[in_hbm, in_smem, in_hbm, in_hbm, in_hbm, in_smem, in_smem],
        out_specs=(in_vmem, in_vmem),
        scratch_shapes=scratch,
        compiler_params=pltpu.CompilerParams(
            collective_id=0, has_side_effects=True, vmem_limit_bytes=60 * 1024 * 1024
        ),
        name="em_iteration",
    )(particles, inv_noise, class_images, col_factor, row_factor, row_shifts, col_shifts)
    return new_averages, occupancy.reshape(OWNED)


def solution(mesh, layout=(4, 4, 4, 2)):
    placed = (
        P(("grp", "own"), None, None),
        P(("grp", "own")),
        P("own", None, None),
        P(),
        P(),
        P(),
        P(),
    )
    return jax.shard_map(
        functools.partial(on_device, layout),
        mesh=mesh,
        in_specs=placed,
        out_specs=(P("own", None), P("own")),
        check_vma=False,
    )
```

```python
import functools

import jax
import jax.numpy as jnp
from jax import lax
from jax.experimental import pallas as pl
from jax.experimental.pallas import tpu as pltpu
from jax.sharding import PartitionSpec as P

F32 = jnp.float32
BF16 = jnp.bfloat16
ANGLES = 128
SHIFTS = 3
FINE = 8
COARSE = ANGLES // FINE
OWNED = 4
SUBS = 4
QUARTERS = 4
POLAR_TILE = 256
CLASS_TILES = 4
SUM_TILE = 512
MESH = pl.DeviceIdType.MESH


def contract_last(left, right):
    return lax.dot_general(left, right, (((1,), (1,)), ((), ())), preferred_element_type=F32)


def matmul(left, right):
    return jnp.dot(left, right, preferred_element_type=F32)


def kernel(
    layout,
    part_hbm,
    noise_ref,
    cls_hbm,
    col_hbm,
    row_hbm,
    rs_ref,
    cs_ref,
    new_ref,
    mass_ref,
    part_ref,
    cls_ref,
    col_ref,
    row_ref,
    pics,
    spread_a,
    spread_b,
    rowp,
    cp_f32,
    cp_block,
    cp_wide,
    cp_all,
    pp_all,
    beta_all,
    stats,
    part_hi,
    part_lo,
    part_ninth,
    cls_roll,
    norm_acc,
    score_a,
    score_b,
    weight_a,
    weight_b,
    grid_a,
    grid_b,
    own_sum,
    x_send,
    x_recv,
    xm_send,
    xm_recv,
    z_send,
    z_recv,
    gathered,
    load_sem,
    pair_send_sem,
    pair_recv_sem,
    cz_send_sem,
    cz_recv_sem,
    cx_send_sem,
    cx_recv_sem,
    x_send_sem,
    x_recv_sem,
    xm_send_sem,
    xm_recv_sem,
    z_send_sem,
    z_recv_sem,
    g_send_sem,
    g_recv_sem,
):
    xs, ys, zhs, zls = layout
    side = part_ref.shape[1]
    polar = col_ref.shape[1]
    cycles = polar // ANGLES
    width = polar // QUARTERS
    quarter_cycles = cycles // QUARTERS
    owners = xs * zhs
    local = OWNED * owners
    block_rows = OWNED * zhs
    y_width = polar // ys
    z_width = y_width // zls

    grp = lax.axis_index("grp")
    own = lax.axis_index("own")
    zl = grp % zls
    y = grp // zls
    core = own % 2
    x = (own // 2) % xs
    zh = own // (2 * xs)

    def device(y_at, zl_at, zh_at, x_at, core_at):
        return {"grp": y_at * zls + zl_at, "own": (zh_at * xs + x_at) * 2 + core_at}

    partner = device(y, zl, zh, x, 1 - core)

    def x_peer(step):
        return device(y, zl, zh, (x + step) % xs, core)

    def plane_peer(back, ahead):
        return device((y + ahead) % ys, zl, zh, (x + xs - back) % xs, core)

    def z_peer(high, low):
        return device(y, (zl + low) % zls, (zh + high) % zhs, x, core)

    def g_peer(step_y, step_l):
        return device((y + step_y) % ys, (zl + step_l) % zls, zh, x, core)

    peers = [partner]
    peers += [
        plane_peer(back, ahead) for back in range(xs) for ahead in range(ys) if back or ahead
    ]
    peers += [z_peer(high, low) for high in range(zhs) for low in range(zls) if high or low]
    peers += [
        g_peer(step_y, step_l) for step_y in range(1, ys) for step_l in range(1, zls)
    ]
    barrier = pltpu.get_barrier_semaphore()
    for peer in peers:
        pl.semaphore_signal(barrier, inc=1, device_id=peer, device_id_type=MESH)

    def chunk_at(turn):
        return pl.multiple_of(((y + turn) % ys) * y_width, y_width)

    cls_load = pltpu.make_async_copy(cls_hbm, cls_ref, load_sem.at[0])
    part_load = pltpu.make_async_copy(part_hbm, part_ref, load_sem.at[1])
    cls_load.start()
    factor_loads = []
    for turn in range(ys):
        cols = pl.ds(chunk_at(turn), y_width)
        pair = [
            pltpu.make_async_copy(col_hbm.at[:, cols], col_ref.at[:, cols], load_sem.at[2 + 2 * turn]),
            pltpu.make_async_copy(row_hbm.at[:, cols], row_ref.at[:, cols], load_sem.at[3 + 2 * turn]),
        ]
        for copy in pair:
            copy.start()
        factor_loads.append(pair)
        if turn == 0:
            part_load.start()

    def remote(src, dst, send_sem, recv_sem, peer):
        return pltpu.make_async_remote_copy(
            src_ref=src,
            dst_ref=dst,
            send_sem=send_sem,
            recv_sem=recv_sem,
            device_id=peer,
            device_id_type=MESH,
        )

    def class_spread(tile, store):
        store[0 : OWNED * side, :] = matmul(
            cls_ref[...].reshape(OWNED * side, side),
            col_ref[:, pl.ds(pl.multiple_of(y * y_width + tile * POLAR_TILE, POLAR_TILE), POLAR_TILE)],
        )

    def class_reduce(tile, store):
        for half in range(POLAR_TILE // ANGLES):
            at = pl.multiple_of(y * y_width + tile * POLAR_TILE + half * ANGLES, ANGLES)
            lanes = slice(half * ANGLES, (half + 1) * ANGLES)
            totals = [jnp.zeros((8, ANGLES), F32)] * OWNED
            for block in range(side // 16):
                rows = row_ref[block * 16 : block * 16 + 16, pl.ds(at, ANGLES)].astype(F32)
                for sub in range(2):
                    for k in range(OWNED):
                        start = k * side + block * 16 + sub * 8
                        totals[k] = totals[k] + store[start : start + 8, lanes] * rows[sub * 8 : sub * 8 + 8]
            for k in range(OWNED):
                cp_f32[tile * OWNED + k : tile * OWNED + k + 1, lanes] = jnp.sum(
                    totals[k], axis=0, keepdims=True
                )

    tiles_per_quarter = width // POLAR_TILE
    last_tile = polar // POLAR_TILE - 1
    cls_load.wait()
    for copy in factor_loads[0]:
        copy.wait()
    spreads = [spread_a, spread_b]
    class_spread(0, spread_a)
    for tile in range(CLASS_TILES):
        if tile + 1 < CLASS_TILES:
            class_spread(tile + 1, spreads[(tile + 1) % 2])
        class_reduce(tile, spreads[tile % 2])
    cp_block[0] = cp_f32[...].astype(BF16)

    pl.semaphore_wait(barrier, len(peers))
    waits = []

    def start(copy):
        copy.start()
        waits.append(copy)
        return copy

    gather_z = [
        start(
            remote(
                cp_block.at[0],
                cp_block.at[high],
                cz_send_sem.at[high],
                cz_recv_sem.at[high],
                z_peer(high, 0),
            )
        )
        for high in range(1, zhs)
    ]
    gather = {}

    def forward():
        for copy in gather_z:
            copy.wait_recv()
        for high in range(zhs):
            block = cp_block[high].astype(F32)
            for tile in range(CLASS_TILES):
                cp_wide[
                    OWNED * high : OWNED * high + OWNED, tile * POLAR_TILE : (tile + 1) * POLAR_TILE
                ] = block[OWNED * tile : OWNED * tile + OWNED]
        cp_all[0, 0] = cp_wide[...].astype(BF16)
        for turn in range(ys):
            for step in range(xs):
                if step or turn:
                    gather[step, turn] = start(
                        remote(
                            cp_all.at[0, 0],
                            cp_all.at[step, turn],
                            cx_send_sem.at[step, turn],
                            cx_recv_sem.at[step, turn],
                            plane_peer(xs - step, ys - turn),
                        )
                    )

    beta_rows = lax.broadcasted_iota(jnp.int32, (8, ANGLES), 0)
    beta_all[core] = jnp.where(beta_rows == 0, noise_ref[0], noise_ref[1])
    beta_copy = start(
        remote(
            beta_all.at[core], beta_all.at[core], pair_send_sem.at[0], pair_recv_sem.at[0], partner
        )
    )

    for pair in factor_loads[1:]:
        for copy in pair:
            copy.wait()
    part_load.wait()
    from_col = lax.broadcasted_iota(jnp.int32, (side, side), 0)
    to_col = lax.broadcasted_iota(jnp.int32, (side, side), 1)
    for j in range(SHIFTS):
        mover = jnp.where(((to_col - cs_ref[j]) & (side - 1)) == from_col, 1.0, 0.0).astype(BF16)
        for n in range(2):
            start_row = (n * SHIFTS + j) * side
            pics[start_row : start_row + side, :] = matmul(part_ref[n], mover).astype(BF16)

    def extend(cycle, carry):
        at = pl.multiple_of(cycle * ANGLES, ANGLES)
        values = row_ref[:, pl.ds(at, ANGLES)].astype(F32)
        rowp[cycle, 8 : side + 8, :] = values
        rowp[cycle, 0:8, :] = values[side - 8 : side]
        rowp[cycle, side + 8 : side + 16, :] = values[0:8]
        return carry

    lax.fori_loop(0, cycles, extend, 0)

    offsets = [rs_ref[i] for i in range(SHIFTS)]

    def part_spread(tile, store):
        store[...] = matmul(
            pics[...],
            col_ref[:, pl.ds(pl.multiple_of(tile * POLAR_TILE, POLAR_TILE), POLAR_TILE)],
        )

    def part_reduce(tile, quarter, store):
        for half in range(POLAR_TILE // ANGLES):
            cycle = tile * (POLAR_TILE // ANGLES) + half
            place = pl.multiple_of((cycle - quarter * quarter_cycles) * ANGLES, ANGLES)
            lanes = slice(half * ANGLES, (half + 1) * ANGLES)
            totals = [jnp.zeros((8, ANGLES), F32)] * (2 * SHIFTS * SHIFTS)
            for block in range(side // 8):
                rows = [
                    rowp[cycle, pl.ds(8 + block * 8 + offsets[i], 8), :] for i in range(SHIFTS)
                ]
                for n in range(2):
                    for j in range(SHIFTS):
                        begin = (n * SHIFTS + j) * side + block * 8
                        value = store[begin : begin + 8, lanes]
                        for i in range(SHIFTS):
                            index = n * 9 + i * SHIFTS + j
                            totals[index] = totals[index] + value * rows[i]
            for n in range(2):
                for s in range(8):
                    pp_all[core, quarter, 8 * n + s : 8 * n + s + 1, pl.ds(place, ANGLES)] = jnp.sum(
                        totals[n * 9 + s], axis=0, keepdims=True
                    )
                ninth = jnp.broadcast_to(
                    jnp.sum(totals[n * 9 + 8], axis=0, keepdims=True), (8, ANGLES)
                )
                for sub in range(SUBS):
                    row = 16 + 2 * sub + n
                    moved = ninth if sub == 0 else pltpu.roll(ninth, sub * FINE, 1)
                    pp_all[core, quarter, row : row + 1, pl.ds(place, ANGLES)] = moved[0:1]

    pair_copies = []
    part_spread(0, spread_a)
    for quarter in range(QUARTERS):

        def part_pair(step, carry):
            tile = quarter * tiles_per_quarter + 2 * step
            part_spread(tile + 1, spread_b)
            part_reduce(tile, quarter, spread_a)
            part_spread(jnp.minimum(tile + 2, last_tile), spread_a)
            part_reduce(tile + 1, quarter, spread_b)
            return carry

        lax.fori_loop(0, tiles_per_quarter // 2, part_pair, 0)
        pair_copies.append(
            start(
                remote(
                    pp_all.at[core, quarter],
                    pp_all.at[core, quarter],
                    pair_send_sem.at[1 + quarter],
                    pair_recv_sem.at[1 + quarter],
                    partner,
                )
            )
        )
        if quarter == 1:
            forward()

    def split_store(value, rows, at, high_ref, low_ref, low_rows):
        high = value.astype(BF16)
        high_ref[rows, pl.ds(at, ANGLES)] = high
        low_ref[low_rows, pl.ds(at, ANGLES)] = (value - high.astype(F32)).astype(BF16)

    ninth_rows = 16 * (COARSE // SUBS)
    for quarter in range(QUARTERS):
        pair_copies[quarter].wait_recv()

        def roll_particles(step, carry):
            lanes = pl.ds(pl.multiple_of(step * ANGLES, ANGLES), ANGLES)
            at = pl.multiple_of(quarter * width + step * ANGLES, ANGLES)
            first = pp_all[0, quarter, :, lanes]
            second = pp_all[1, quarter, :, lanes]
            eight = jnp.concatenate([first[0:16], second[0:16]], axis=0)
            ninth = jnp.concatenate([first[16:24], second[16:24]], axis=0)
            for coarse in range(COARSE):
                moved = eight if coarse == 0 else pltpu.roll(eight, coarse * FINE, 1)
                rows = slice(32 * coarse, 32 * coarse + 32)
                split_store(moved, rows, at, part_hi, part_lo, rows)
            for coarse in range(COARSE // SUBS):
                moved = ninth if coarse == 0 else pltpu.roll(ninth, coarse * FINE * SUBS, 1)
                rows = slice(16 * coarse, 16 * coarse + 16)
                low_rows = slice(ninth_rows + 16 * coarse, ninth_rows + 16 * coarse + 16)
                split_store(moved, rows, at, part_ninth, part_ninth, low_rows)
            return carry

        [roll_particles(step, 0) for step in range(quarter_cycles)]

    norm_acc[...] = jnp.zeros_like(norm_acc)

    def roll_classes(turn):
        for step in range(xs):
            if step or turn:
                gather[step, turn].wait_recv()
        norm = norm_acc[...]
        for cycle in range(y_width // ANGLES):
            lanes = slice(cycle * ANGLES, (cycle + 1) * ANGLES)
            at = slice(turn * y_width + cycle * ANGLES, turn * y_width + (cycle + 1) * ANGLES)
            rows = cp_all[:, turn, :, lanes].astype(F32).reshape(local, ANGLES)
            norm = norm + rows * rows
            for fine in range(FINE):
                moved = rows if fine == 0 else pltpu.roll(rows, ANGLES - fine, 1)
                cls_roll[fine * local : (fine + 1) * local, at] = moved.astype(BF16)
        norm_acc[...] = norm

    for turn in range(ys):
        roll_classes(turn)
        classes = cls_roll[:, turn * y_width : (turn + 1) * y_width]
        cols = pl.ds(chunk_at(turn), y_width)
        eight = contract_last(classes, part_hi[:, cols]) + contract_last(classes, part_lo[:, cols])
        ninth = contract_last(classes, part_ninth[:, cols])
        if turn == 0:
            score_a[...] = eight
            score_b[...] = ninth
        else:
            score_a[...] += eight
            score_b[...] += ninth

    beta_copy.wait_recv()
    half_norm = 0.5 * jnp.sum(norm_acc[...], axis=1, keepdims=True)
    half_norm = jnp.concatenate([half_norm] * FINE, axis=0)
    lane_a = lax.broadcasted_iota(jnp.int32, (1, 32 * COARSE), 1)
    lane_b = lax.broadcasted_iota(jnp.int32, (1, 2 * ninth_rows), 1)
    who_a = (lane_a // 8) % 4
    who_b = ((lane_b // 8) % 2) * 2 + lane_b % 2
    first_b = lane_b < ninth_rows

    def along(values, who):
        return jnp.where(
            who == 0, values[0], jnp.where(who == 1, values[1], jnp.where(who == 2, values[2], values[3]))
        )

    betas = [beta_all[p // 2, p % 2 : p % 2 + 1, 0:1] for p in range(4)]
    full_b = score_b[...]
    full_b = full_b + pltpu.roll(full_b, ninth_rows, 1)
    full_a = along(betas, who_a) * (score_a[...] - half_norm)
    full_b = along(betas, who_b) * (full_b - half_norm)
    top_a = jnp.max(full_a, axis=0, keepdims=True)
    top_b = jnp.max(full_b, axis=0, keepdims=True)
    low = jnp.float32(-jnp.inf)

    def pick_max(p):
        return jnp.maximum(
            jnp.max(jnp.where(who_a == p, top_a, low), axis=1, keepdims=True),
            jnp.max(jnp.where(who_b == p, top_b, low), axis=1, keepdims=True),
        )

    tops = [pick_max(p) for p in range(4)]
    raised_a = jnp.exp(full_a - along(tops, who_a))
    raised_b = jnp.exp(full_b - along(tops, who_b))
    score_a[...] = raised_a
    score_b[...] = raised_b
    total_a = jnp.sum(raised_a, axis=0, keepdims=True)
    total_b = jnp.sum(raised_b, axis=0, keepdims=True)

    def pick_sum(p):
        return jnp.sum(jnp.where(who_a == p, total_a, 0.0), axis=1, keepdims=True) + jnp.sum(
            jnp.where((who_b == p) & first_b, total_b, 0.0), axis=1, keepdims=True
        )

    parts = [pick_sum(p) for p in range(4)]
    for p in range(4):
        stats[0, p : p + 1, :] = jnp.broadcast_to(tops[p], (1, ANGLES))
        stats[0, p + 4 : p + 5, :] = jnp.broadcast_to(parts[p], (1, ANGLES))
    stat_copy = start(
        remote(
            stats.at[0],
            stats.at[1],
            pair_send_sem.at[1 + QUARTERS],
            pair_recv_sem.at[1 + QUARTERS],
            partner,
        )
    )
    stat_copy.wait_recv()
    factors = []
    for p in range(4):
        other_top = stats[1, p : p + 1, 0:1]
        other_part = stats[1, p + 4 : p + 5, 0:1]
        top = jnp.maximum(tops[p], other_top)
        mine = jnp.exp(tops[p] - top)
        factors.append(mine / (parts[p] * mine + other_part * jnp.exp(other_top - top)))
    final_a = score_a[...] * along(factors, who_a)
    final_b = score_b[...] * along(factors, who_b)
    weight_a[...] = final_a.astype(BF16)
    weight_b[...] = final_b.astype(BF16)
    lane_sum = jnp.where(first_b, final_b, 0.0)
    for piece in range(32 * COARSE // ANGLES):
        lane_sum = lane_sum + final_a[:, piece * ANGLES : (piece + 1) * ANGLES]
    mass = lane_sum[0:local]
    for fine in range(1, FINE):
        mass = mass + lane_sum[fine * local : (fine + 1) * local]
    mass = jnp.broadcast_to(jnp.sum(mass, axis=1, keepdims=True), (local, ANGLES))
    for step in range(xs):
        xm_send[step] = mass[step * block_rows : (step + 1) * block_rows]

    def ahead_of(turn):
        if ys == 4:
            return (2 + turn + (turn // 2) * (1 + 2 * (turn % 2))) % 4
        return ys - 1 - turn

    def plane_copy(back, turn, side_at):
        return remote(
            x_send.at[back, turn, side_at],
            x_recv.at[back, turn, side_at],
            x_send_sem.at[back, turn, side_at],
            x_recv_sem.at[back, turn, side_at],
            plane_peer(back, ahead_of(turn)),
        )

    mass_copies = [
        start(
            remote(
                xm_send.at[back],
                xm_recv.at[back],
                xm_send_sem.at[back],
                xm_recv_sem.at[back],
                plane_peer(back, 0),
            )
        )
        for back in range(1, xs)
    ]

    def weigh(tile, store):
        cols = pl.ds(pl.multiple_of(tile * SUM_TILE, SUM_TILE), SUM_TILE)
        store[...] = matmul(weight_a[...], part_hi[:, cols]) + matmul(
            weight_b[...], part_ninth[:, cols]
        )

    def unroll(turn, side_at, first, store):
        for piece in range(SUM_TILE // ANGLES):
            lanes = slice(piece * ANGLES, (piece + 1) * ANGLES)
            total = store[0:local, lanes]
            for fine in range(1, FINE):
                total = total + pltpu.roll(store[fine * local : (fine + 1) * local, lanes], fine, 1)
            if first:
                own_sum[side_at, :, lanes] = total[0:block_rows]
            for back in range(first, xs):
                x_send[back, turn, side_at, :, lanes] = total[
                    back * block_rows : (back + 1) * block_rows
                ].astype(BF16)
        for back in range(first, xs):
            plane_copy(back, turn, side_at).start()

    def tile_of(turn):
        return 2 * ((y + ahead_of(turn)) % ys)

    weigh(tile_of(0), grid_a)

    def sum_pair(turn, carry):
        weigh(tile_of(turn) + 1, grid_b)
        unroll(turn, 0, 0, grid_a)
        weigh(tile_of(turn + 1), grid_a)
        unroll(turn, 1, 0, grid_b)
        return carry

    lax.fori_loop(0, ys - 1, sum_pair, 0)
    weigh(2 * y + 1, grid_b)
    unroll(ys - 1, 0, 1, grid_a)
    unroll(ys - 1, 1, 1, grid_b)

    mass = xm_send[0]
    for back in range(1, xs):
        mass_copies[back - 1].wait_recv()
        mass = mass + xm_recv[back]
    halves = []
    for side_at in range(2):
        total = own_sum[side_at]
        for turn in range(ys):
            for back in range(xs):
                if back or turn != ys - 1:
                    plane_copy(back, turn, side_at).wait_recv()
                    total = total + x_recv[back, turn, side_at].astype(F32)
        halves.append(total)
    total = jnp.concatenate(halves + [mass], axis=1)
    for high in range(zhs):
        rows = total[OWNED * high : OWNED * high + OWNED]
        for low_at in range(zls):
            z_send[high, low_at, :, 0:z_width] = rows[:, low_at * z_width : (low_at + 1) * z_width]
            z_send[high, low_at, :, z_width : z_width + ANGLES] = rows[:, y_width : y_width + ANGLES]
    z_copies = [
        start(
            remote(
                z_send.at[high, (zl + low_at) % zls],
                z_recv.at[high, low_at],
                z_send_sem.at[high, low_at],
                z_recv_sem.at[high, low_at],
                z_peer(zhs - high, low_at),
            )
        )
        for high in range(zhs)
        for low_at in range(zls)
        if high or low_at
    ]
    total = z_send[0, zl]
    slots = [(high, low_at) for high in range(zhs) for low_at in range(zls) if high or low_at]
    for copy, (high, low_at) in zip(z_copies, slots):
        copy.wait_recv()
        total = total + z_recv[high, low_at]
    gathered[grp] = total
    g_copies = [
        start(
            remote(
                gathered.at[grp],
                gathered.at[grp],
                g_send_sem.at[step_y, step_l],
                g_recv_sem.at[step_y, step_l],
                g_peer(step_y, step_l),
            )
        )
        for step_y in range(ys)
        for step_l in range(zls)
        if step_y or step_l
    ]
    for turn in range(ys):
        for back in range(xs):
            if back or turn != ys - 1:
                for side_at in range(2):
                    plane_copy(back, turn, side_at).wait_send()
    for copy in g_copies:
        copy.wait_recv()
    mass = gathered[0, :, z_width : z_width + ANGLES]
    for part in range(1, ys):
        mass = mass + gathered[part * zls, :, z_width : z_width + ANGLES]
    on_diagonal = lax.broadcasted_iota(jnp.int32, (OWNED, ANGLES), 0) == lax.broadcasted_iota(
        jnp.int32, (OWNED, ANGLES), 1
    )
    mass_ref[...] = jnp.sum(jnp.where(on_diagonal, mass, 0.0), axis=0, keepdims=True)[:, 0:OWNED]
    divisor = jnp.maximum(mass[:, 0:1], 1.0)
    for part in range(ys * zls):
        new_ref[:, part * z_width : (part + 1) * z_width] = gathered[part, :, 0:z_width] / divisor
    for copy in waits:
        copy.wait_send()


def on_device(layout, particles, inv_noise, class_images, col_factor, row_factor, row_shifts, col_shifts):
    xs, ys, zhs, zls = layout
    side = particles.shape[1]
    polar = col_factor.shape[1]
    cycles = polar // ANGLES
    width = polar // QUARTERS
    local = OWNED * xs * zhs
    block_rows = OWNED * zhs
    y_width = polar // ys
    z_width = y_width // zls
    eight = 32 * COARSE
    ninth = 2 * 16 * (COARSE // SUBS)
    vmem = pltpu.VMEM
    dma = pltpu.SemaphoreType.DMA
    scratch = [
        vmem((2, side, side), BF16),
        vmem((OWNED, side, side), BF16),
        vmem((side, polar), BF16),
        vmem((side, polar), BF16),
        vmem((2 * SHIFTS * side, side), BF16),
        vmem((2 * SHIFTS * side, POLAR_TILE), F32),
        vmem((2 * SHIFTS * side, POLAR_TILE), F32),
        vmem((cycles, side + 16, ANGLES), F32),
        vmem((OWNED * CLASS_TILES, POLAR_TILE), F32),
        vmem((zhs, OWNED * CLASS_TILES, POLAR_TILE), BF16),
        vmem((block_rows, y_width), F32),
        vmem((xs, ys, block_rows, y_width), BF16),
        vmem((2, QUARTERS, 24, width), F32),
        vmem((2, 8, ANGLES), F32),
        vmem((2, 8, ANGLES), F32),
        vmem((eight, polar), BF16),
        vmem((eight, polar), BF16),
        vmem((ninth, polar), BF16),
        vmem((FINE * local, polar), BF16),
        vmem((local, ANGLES), F32),
        vmem((FINE * local, eight), F32),
        vmem((FINE * local, ninth), F32),
        vmem((FINE * local, eight), BF16),
        vmem((FINE * local, ninth), BF16),
        vmem((FINE * local, SUM_TILE), F32),
        vmem((FINE * local, SUM_TILE), F32),
        vmem((2, block_rows, SUM_TILE), F32),
        vmem((xs, ys, 2, block_rows, SUM_TILE), BF16),
        vmem((xs, ys, 2, block_rows, SUM_TILE), BF16),
        vmem((xs, block_rows, ANGLES), F32),
        vmem((xs, block_rows, ANGLES), F32),
        vmem((zhs, zls, OWNED, z_width + ANGLES), F32),
        vmem((zhs, zls, OWNED, z_width + ANGLES), F32),
        vmem((ys * zls, OWNED, z_width + ANGLES), F32),
        dma((2 + 2 * ys,)),
        dma((2 + QUARTERS,)),
        dma((2 + QUARTERS,)),
        dma((zhs,)),
        dma((zhs,)),
        dma((xs, ys)),
        dma((xs, ys)),
        dma((xs, ys, 2)),
        dma((xs, ys, 2)),
        dma((xs,)),
        dma((xs,)),
        dma((zhs, zls)),
        dma((zhs, zls)),
        dma((ys, zls)),
        dma((ys, zls)),
    ]
    in_vmem = pl.BlockSpec(memory_space=pltpu.VMEM)
    in_smem = pl.BlockSpec(memory_space=pltpu.SMEM)
    in_hbm = pl.BlockSpec(memory_space=pl.ANY)
    new_averages, occupancy = pl.pallas_call(
        functools.partial(kernel, layout),
        out_shape=(
            jax.ShapeDtypeStruct((OWNED, polar), F32),
            jax.ShapeDtypeStruct((1, OWNED), F32),
        ),
        in_specs=[in_hbm, in_smem, in_hbm, in_hbm, in_hbm, in_smem, in_smem],
        out_specs=(in_vmem, in_vmem),
        scratch_shapes=scratch,
        compiler_params=pltpu.CompilerParams(
            collective_id=0, has_side_effects=True, vmem_limit_bytes=60 * 1024 * 1024
        ),
        name="em_iteration",
    )(particles, inv_noise, class_images, col_factor, row_factor, row_shifts, col_shifts)
    return new_averages, occupancy.reshape(OWNED)


def solution(mesh, layout=(4, 4, 4, 2)):
    placed = (
        P(("grp", "own"), None, None),
        P(("grp", "own")),
        P("own", None, None),
        P(),
        P(),
        P(),
        P(),
    )
    return jax.shard_map(
        functools.partial(on_device, layout),
        mesh=mesh,
        in_specs=placed,
        out_specs=(P("own", None), P("own")),
        check_vma=False,
    )
```
